32 devices in a mesh: dp: 8 (over z, y), tensor: 4 (over x, core).
Axes of the slice: x: 2, y: 2, z: 4, core: 2. Of those that a mesh axis runs over, the one named last changes fastest.
Arguments:
- inputs: bfloat16 [4096, 5120], P('dp', 'tensor'), may hold values from -6 to 6
- cotangent: bfloat16 [4096, 1024], P('dp', 'tensor'), may hold values from -1.5 to 1.5
- base_weight: bfloat16 [5120, 1024], P('tensor'), may hold values from -0.078125 to 0.078125
- down_a: bfloat16 [16, 5120, 16], P('dp', 'tensor'), may hold values from -0.078125 to 0.078125
- up_b: bfloat16 [16, 16, 1024], P('dp', None, 'tensor'), may hold values from -1.5 to 1.5
- block_adapter: int32 [32], P('dp'), may hold values from 0 to 15, as said below
- token_adapter: int32 [4096], P('dp'), may hold values from -1 to 15, as said below
- owner_map: int32 [16], replicated, may hold values from 0 to 15, each once
Outputs:
- gradient_wrt_input: bfloat16 [4096, 5120], P('dp', 'tensor')
- grad_b: float32 [16, 16, 1024], P('dp', None, 'tensor')
The draws below stay inside these ranges and needn't reach their ends.
Inputs may be any that keep to these rules, and one draw needn't show every extreme that they name: `block_adapter`: each block of 128 rows serves one adapter; some adapters serve many blocks. `token_adapter`: in each block the first rows (at least 32 of them) carry the block's adapter and the rest are padding with -1. A permutation; adapter e stands at slot owner_map[e], on dp index owner_map[e] // 2.
All inputs are finite; a program needn't handle non-finite values.
Results may differ from the reference program's by a relative error of at most 0.0045.
Values may be sent and summed in bfloat16 or wider, within the bound.
A program may use at most 64 MiB of HBM per device.

```python
import jax
import jax.numpy as jnp
from jax import lax

D = 5120
RANK = 16
BLK = 128
KOUT = 1024
ADAPTERS = 16
BLOCKS = 32
TOKENS = 4096


def block_choice(key):
    first, second, third, mixer = jax.random.split(key, 4)
    picked = jax.random.randint(first, (BLOCKS,), 0, ADAPTERS)
    picked = jnp.minimum(picked, jax.random.randint(second, (BLOCKS,), 0, ADAPTERS))
    picked = jnp.minimum(picked, jax.random.randint(third, (BLOCKS,), 0, ADAPTERS))
    relabel = jax.random.permutation(mixer, ADAPTERS)
    return relabel[picked].astype(jnp.int32)


def draw_block_adapter(key, part):
    block_ids = block_choice(key)
    return block_ids


def draw_token_adapter(key, part):
    block_ids = block_choice(key)
    key = jax.random.fold_in(key, 7)
    live_counts = jax.random.randint(key, (BLOCKS,), BLK // 4, BLK + 1)
    position = jnp.arange(BLK, dtype=jnp.int32)[None, :]
    labels = jnp.where(position < live_counts[:, None], block_ids[:, None], -1)
    return labels.reshape(BLOCKS * BLK).astype(jnp.int32)


def block_levels(stream_key, extent, shards, smallest, largest):
    def one(axis_at, shards_of):
        steps = jax.random.uniform(jax.random.fold_in(jax.random.fold_in(stream_key, 6), axis_at), (shards_of,), jnp.float32, smallest / len(shards), largest / len(shards))
        return jnp.repeat(jnp.exp(steps), extent[axis_at] // shards_of).reshape((-1,) + (1,) * (len(extent) - axis_at - 1))

    gain = one(*shards[0])
    for cut in shards[1:]:
        gain = gain * one(*cut)
    return gain


def centred(stream_key, shape, width, bound, shards=(), kind=jnp.bfloat16):
    values = width * jax.random.normal(stream_key, shape, jnp.float32)
    if shards:
        values = values * block_levels(stream_key, shape, shards, -0.22, 0.18)
    return jnp.clip(values, -bound, bound).astype(kind)


def setup_inputs(seed: int = 0) -> dict:
    keys = jax.random.split(jax.random.key(seed), 9)
    return {
        "inputs": centred(keys[0], (TOKENS, D), 1.0, 6.0, ((0, 8), (1, 4))),
        "cotangent": centred(keys[1], (TOKENS, KOUT), 0.25, 1.5, ((0, 8), (1, 4))),
        "base_weight": centred(keys[2], (D, KOUT), D ** -0.5, 0.078125, ((0, 4),)),
        "down_a": centred(keys[3], (ADAPTERS, D, RANK), D ** -0.5, 0.078125, ((0, 8), (1, 4))),
        "up_b": centred(keys[4], (ADAPTERS, RANK, KOUT), RANK ** -0.5, 1.5, ((0, 8), (2, 4))),
        "block_adapter": draw_block_adapter(jax.random.fold_in(keys[8], 71), 0),
        "token_adapter": draw_token_adapter(jax.random.fold_in(keys[8], 71), 0),
        "owner_map": jax.random.permutation(keys[7], ADAPTERS).astype(jnp.int32),
    }


adapter_scale_factor = 2.0


def reference(inputs, cotangent, base_weight, down_a, up_b, block_adapter, token_adapter, owner_map):
    slot_ids = owner_map[block_adapter].astype(jnp.int32)
    live_rows = (token_adapter >= 0).astype(jnp.float32).reshape(BLOCKS, BLK, 1)
    input_row_blocks = inputs.reshape(BLOCKS, BLK, D)
    g_blocks = cotangent.reshape(BLOCKS, BLK, KOUT)
    contract_last = (((1,), (1,)), ((), ()))

    def one_block(operands):
        x_block, g_block, mask_block, slot = operands
        selected_down_matrix = lax.dynamic_index_in_dim(down_a, slot, 0, keepdims=False)
        up_sel = lax.dynamic_index_in_dim(up_b, slot, 0, keepdims=False)
        low_rank_product = (jnp.dot(x_block, selected_down_matrix, preferred_element_type=jnp.float32) * mask_block).astype(jnp.bfloat16)
        masked_rows = (g_block.astype(jnp.float32) * mask_block).astype(jnp.bfloat16)
        hidden_features = lax.dot_general(masked_rows, up_sel, contract_last, preferred_element_type=jnp.float32).astype(jnp.bfloat16)
        frozen_path_gradient = lax.dot_general(masked_rows, base_weight, contract_last, preferred_element_type=jnp.float32)
        adapter_path_gradient = lax.dot_general(hidden_features, selected_down_matrix, contract_last, preferred_element_type=jnp.float32)
        block_input_gradient = (frozen_path_gradient + adapter_scale_factor * adapter_path_gradient).astype(jnp.bfloat16)
        block_partial_term = adapter_scale_factor * jnp.dot(low_rank_product.T, masked_rows, preferred_element_type=jnp.float32)
        return block_input_gradient, block_partial_term

    grads, block_partial_terms = lax.map(one_block, (input_row_blocks, g_blocks, live_rows, slot_ids))
    grad_b = jnp.zeros((ADAPTERS, RANK, KOUT), jnp.float32).at[slot_ids].add(block_partial_terms)
    return grads.reshape(TOKENS, D), grad_b
```

```python
import functools

import jax
import jax.numpy as jnp
from jax import lax
from jax.experimental import pallas as pl
from jax.experimental.pallas import tpu as pltpu
from jax.sharding import PartitionSpec as P

adapter_scale_factor = 2.0
MESH = pl.DeviceIdType.MESH
LAST = (((1,), (1,)), ((), ()))
FIRST = (((0,), (0,)), ((), ()))


def loop(lo, hi, body):
    if hi - lo <= 8:
        for i in range(lo, hi):
            body(i)
    else:
        lax.fori_loop(lo, hi, lambda i, c: (body(i), c)[1], 0)


def kernel(
    ndp, nten, owner_ref, block_ref, tok_ref, x_ref, g_ref, w_ref, a_ref, u_ref,
    out_ref, grad_ref,
    xv, wv, gall, gm, aall, uall, part, sib, chip, outv, gsend, grecv,
    local_sem, out_sem, a_send, a_recv, g_xsend, g_ssend, g_recv,
    p_send, p_recv, c_send, c_recv, r_send, r_recv,
):
    nblk = block_ref.shape[0]
    rows, dpiece = x_ref.shape
    kpiece = g_ref.shape[1]
    brows = rows // nblk
    own = a_ref.shape[0]
    inner = 2 if ndp % 2 == 0 else 1
    outer = ndp // inner
    nx = nten // 2
    me, t = lax.axis_index("dp"), lax.axis_index("tensor")
    z, y = lax.div(me, inner), lax.rem(me, inner)
    xx, c = lax.div(t, 2), lax.rem(t, 2)
    twin = 2 * xx + 1 - c

    mine = pl.ds(me * own, own)
    local = [
        pltpu.make_async_copy(u_ref, uall.at[mine], local_sem.at[0]),
        pltpu.make_async_copy(a_ref, aall.at[mine], local_sem.at[1]),
        pltpu.make_async_copy(g_ref, gall.at[t], local_sem.at[2]),
        pltpu.make_async_copy(x_ref, xv, local_sem.at[3]),
        pltpu.make_async_copy(w_ref, wv, local_sem.at[4]),
    ]
    for cp in local:
        cp.start()

    barrier = pltpu.get_barrier_semaphore()

    def greet_dp(j):
        pl.semaphore_signal(
            barrier, inc=1, device_id=(lax.rem(me + j, ndp), t), device_id_type=MESH
        )

    def greet_ten(j):
        pl.semaphore_signal(
            barrier, inc=1, device_id=(me, lax.rem(t + j, nten)), device_id_type=MESH
        )

    loop(1, ndp, greet_dp)
    loop(1, nten, greet_ten)
    pl.semaphore_wait(barrier, ndp + nten - 2)

    def hop(src, way, first):
        at = pl.ds(src * own, own)
        if way == 2:
            to = inner * z + 1 - y
        else:
            to = inner * (z + 1 - 2 * way) + y
        return [
            pltpu.make_async_remote_copy(
                src_ref=(ref if first else full.at[at]),
                dst_ref=full.at[at],
                send_sem=a_send.at[i, way, src],
                recv_sem=a_recv.at[i, src],
                device_id=(to, t),
                device_id_type=MESH,
            )
            for i, (ref, full) in enumerate(((a_ref, aall), (u_ref, uall)))
        ]

    def for_ways(fn, ways):
        for way in ways:
            if way == 2:
                if inner == 2:
                    fn(2)
            else:
                ok = z + 1 < outer if way == 0 else z > 0
                pl.when(ok)(functools.partial(fn, way))

    def start_hops(src, ways, first=False):
        def go(way):
            for cp in hop(src, way, first):
                cp.start()

        for_ways(go, ways)

    def wait_hops(src, ways, first=False):
        def go(way):
            for cp in hop(src, way, first):
                cp.wait_send()

        for_ways(go, ways)

    def got_hop(src):
        for cp in hop(src, 0, False):
            cp.wait_recv()

    def line(k, fn):
        pl.when(z - k >= 0)(lambda: fn(inner * (z - k) + y, (0, 2)))
        pl.when(z + k < outer)(lambda: fn(inner * (z + k) + y, (1, 2)))

    def piece(src, i):
        return gall.at[src, pl.ds(i * brows, brows)]

    def g_across(j, i):
        return pltpu.make_async_remote_copy(
            src_ref=g_ref.at[pl.ds(i * brows, brows)],
            dst_ref=piece(t, i),
            send_sem=g_xsend.at[j, i],
            recv_sem=g_recv.at[t, i],
            device_id=(me, 2 * lax.rem(xx + j, nx) + c),
            device_id_type=MESH,
        )

    def g_twin(src, i, first=False):
        return pltpu.make_async_remote_copy(
            src_ref=(g_ref.at[pl.ds(i * brows, brows)] if first else piece(src, i)),
            dst_ref=piece(src, i),
            send_sem=g_ssend.at[src, i],
            recv_sem=g_recv.at[src, i],
            device_id=(me, twin),
            device_id_type=MESH,
        )

    def from_x(j):
        return 2 * lax.rem(xx + j, nx) + c

    start_hops(me, (0, 1, 2), True)
    for i in range(nblk):
        for j in range(1, nx):
            g_across(j, i).start()
        g_twin(t, i, True).start()

    def pass_on(src, ways):
        got_hop(src)
        start_hops(src, ways)

    def pass_g(i):
        for j in range(1, nx):
            g_twin(from_x(j), i).wait_recv()
            g_twin(from_x(j), i).start()

    if outer <= 4:
        for k in range(1, max(outer, nblk + 1)):
            if k < outer:
                line(k, pass_on)
            if k <= nblk:
                pass_g(k - 1)
    else:
        loop(1, outer, lambda k: line(k, pass_on))
        for i in range(nblk):
            pass_g(i)

    live = (tok_ref[...] >= 0).astype(jnp.float32)
    tall = []
    for b in range(nblk):
        lane = live[:, b * brows:(b + 1) * brows]
        col = jnp.broadcast_to(lane, (brows, brows)).T.astype(jnp.bfloat16)
        reps = -(-kpiece // brows)
        tall.append(jnp.concatenate([col] * reps, axis=1)[:, :kpiece])
    slots = [owner_ref[block_ref[b]] for b in range(nblk)]

    for cp in local:
        cp.wait()
    if inner == 2:
        loop(0, outer, lambda k: got_hop(inner * k + 1 - y))

    for b in range(nblk):
        span = slice(b * brows, (b + 1) * brows)
        part[0, :, span] = lax.dot_general(
            aall[slots[b]], xv[span, :], LAST, preferred_element_type=jnp.float32
        )
        part[1, :, span] = lax.dot_general(
            uall[slots[b]], gall[t, span, :], LAST, preferred_element_type=jnp.float32
        )
    to_twin = pltpu.make_async_remote_copy(
        src_ref=part, dst_ref=sib, send_sem=p_send, recv_sem=p_recv,
        device_id=(me, twin), device_id_type=MESH,
    )
    to_twin.start()
    to_twin.wait_recv()
    chip[0] = part[...] + sib[...]

    def to_chip(j):
        return pltpu.make_async_remote_copy(
            src_ref=chip.at[0], dst_ref=chip.at[j],
            send_sem=c_send.at[j], recv_sem=c_recv.at[j],
            device_id=(me, from_x(j)), device_id_type=MESH,
        )

    for j in range(1, nx):
        to_chip(j).start()

    for b in range(nblk):
        span = slice(b * brows, (b + 1) * brows)
        for j in range(1, nx):
            g_twin(2 * lax.rem(xx + j, nx) + 1 - c, b).wait_recv()
        g_twin(twin, b).wait_recv()
        for s in range(nten):
            gm[span, s * kpiece:(s + 1) * kpiece] = gall[s, span, :] * tall[b]

    total = chip[0]
    for j in range(1, nx):
        to_chip(j).wait_recv()
        total = total + chip[j]
    lowrank = (total[0] * live).astype(jnp.bfloat16)
    hidden = (total[1] * live).astype(jnp.bfloat16) * jnp.bfloat16(adapter_scale_factor)

    terms = []
    for b in range(nblk):
        span = slice(b * brows, (b + 1) * brows)
        terms.append(
            adapter_scale_factor
            * jnp.dot(lowrank[:, span], gall[t, span, :], preferred_element_type=jnp.float32)
        )

    def share(owner, s):
        acc = jnp.zeros_like(terms[0])
        for b in range(nblk):
            acc = acc + jnp.where(slots[b] == owner * own + s, terms[b], 0.0)
        return acc

    def to_owner(j):
        return pltpu.make_async_remote_copy(
            src_ref=gsend.at[j], dst_ref=grecv.at[j],
            send_sem=r_send.at[j], recv_sem=r_recv.at[j],
            device_id=(lax.rem(me + j, ndp), t), device_id_type=MESH,
        )

    def scatter(j):
        for s in range(own):
            gsend[j, s] = share(lax.rem(me + j, ndp), s).astype(jnp.bfloat16)
        to_owner(j).start()

    loop(1, ndp, scatter)
    for s in range(own):
        grad_ref[s] = share(me, s)

    tile = 256 if dpiece % 256 == 0 else 128
    outs = []
    for n in range(dpiece // tile):
        cols = slice(n * tile, (n + 1) * tile)
        base = lax.dot_general(gm[...], wv[cols, :], LAST, preferred_element_type=jnp.float32)
        for b in range(nblk):
            span = slice(b * brows, (b + 1) * brows)
            low = lax.dot_general(
                hidden[:, span], aall[slots[b], :, cols], FIRST,
                preferred_element_type=jnp.float32,
            )
            outv[span, cols] = (base[span] + low).astype(jnp.bfloat16)
        cp = pltpu.make_async_copy(outv.at[:, cols], out_ref.at[:, cols], out_sem.at[n])
        cp.start()
        outs.append(cp)

    def gather_grad(j):
        to_owner(j).wait_recv()
        grad_ref[...] += grecv[j].astype(jnp.float32)

    loop(1, ndp, gather_grad)

    for cp in outs:
        cp.wait()
    wait_hops(me, (0, 1, 2), True)
    loop(1, outer, lambda k: line(k, wait_hops))
    for i in range(nblk):
        for j in range(1, nx):
            g_across(j, i).wait_send()
            g_twin(from_x(j), i).wait_send()
        g_twin(t, i, True).wait_send()
    to_twin.wait_send()
    for j in range(1, nx):
        to_chip(j).wait_send()
    loop(1, ndp, lambda j: to_owner(j).wait_send())


def on_device(
    ndp, nten, inputs, cotangent, base_weight, down_a, up_b, block_adapter, token_adapter, owner_map
):
    rows, dpiece = inputs.shape
    kpiece = cotangent.shape[1]
    nblk = block_adapter.shape[0]
    own, rank = up_b.shape[:2]
    slots = own * ndp
    kout = base_weight.shape[1]
    nx = nten // 2
    tile = 256 if dpiece % 256 == 0 else 128
    bf16, f32 = jnp.bfloat16, jnp.float32
    smem = pl.BlockSpec(memory_space=pltpu.SMEM)
    vmem = pl.BlockSpec(memory_space=pltpu.VMEM)
    hbm = pl.BlockSpec(memory_space=pl.ANY)
    dma = pltpu.SemaphoreType.DMA
    return pl.pallas_call(
        functools.partial(kernel, ndp, nten),
        out_shape=(
            jax.ShapeDtypeStruct((rows, dpiece), bf16),
            jax.ShapeDtypeStruct((own, rank, kpiece), f32),
        ),
        in_specs=[smem, smem, vmem, hbm, hbm, hbm, hbm, hbm],
        out_specs=(hbm, vmem),
        scratch_shapes=[
            pltpu.VMEM((rows, dpiece), bf16),
            pltpu.VMEM((dpiece, kout), bf16),
            pltpu.VMEM((nten, rows, kpiece), bf16),
            pltpu.VMEM((rows, kout), bf16),
            pltpu.VMEM((slots, rank, dpiece), bf16),
            pltpu.VMEM((slots, rank, kpiece), bf16),
            pltpu.VMEM((2, rank, rows), f32),
            pltpu.VMEM((2, rank, rows), f32),
            pltpu.VMEM((nx, 2, rank, rows), f32),
            pltpu.VMEM((rows, dpiece), bf16),
            pltpu.VMEM((ndp, own, rank, kpiece), bf16),
            pltpu.VMEM((ndp, own, rank, kpiece), bf16),
            dma((5,)),
            dma((dpiece // tile,)),
            dma((2, 3, ndp)),
            dma((2, ndp)),
            dma((nx, nblk)),
            dma((nten, nblk)),
            dma((nten, nblk)),
            dma,
            dma,
            dma((nx,)),
            dma((nx,)),
            dma((ndp,)),
            dma((ndp,)),
        ],
        cost_estimate=pl.CostEstimate(
            flops=2 * rows * dpiece * (kout + 2 * rank),
            bytes_accessed=2 * (2 * rows * dpiece + dpiece * kout + rows * kpiece),
            transcendentals=0,
        ),
        compiler_params=pltpu.CompilerParams(
            collective_id=0, has_side_effects=True, vmem_limit_bytes=48 * 2**20
        ),
    )(
        owner_map, block_adapter, token_adapter.reshape(1, rows), inputs, cotangent, base_weight,
        jnp.swapaxes(down_a, 1, 2), up_b,
    )


def solution(mesh):
    in_specs = (
        P("dp", "tensor"),
        P("dp", "tensor"),
        P("tensor", None),
        P("dp", "tensor", None),
        P("dp", None, "tensor"),
        P("dp"),
        P("dp"),
        P(),
    )
    out_specs = (P("dp", "tensor"), P("dp", None, "tensor"))
    return jax.shard_map(
        functools.partial(on_device, mesh.shape["dp"], mesh.shape["tensor"]),
        mesh=mesh, in_specs=in_specs, out_specs=out_specs, check_vma=False,
    )
```

```python
import functools

import jax
import jax.numpy as jnp
from jax import lax
from jax.experimental import pallas as pl
from jax.experimental.pallas import tpu as pltpu
from jax.sharding import PartitionSpec as P

adapter_scale_factor = 2.0
MESH = pl.DeviceIdType.MESH
LAST = (((1,), (1,)), ((), ()))
FIRST = (((0,), (0,)), ((), ()))


def loop(lo, hi, body):
    if hi - lo <= 8:
        for i in range(lo, hi):
            body(i)
    else:
        lax.fori_loop(lo, hi, lambda i, c: (body(i), c)[1], 0)


def kernel(
    ndp, nten, owner_ref, block_ref, tok_ref, x_ref, g_ref, w_ref, a_ref, u_ref,
    out_ref, grad_ref,
    owner, block, tok, xv, wv, gall, gm, acc, aall, uall, part, outv, gsend, grecv,
    local_sem, w_sem, out_sem, a_send, a_recv, g_send, g_fwd, g_recv,
    p_send, p_recv, r_send, r_recv,
):
    nblk = block_ref.shape[0]
    rows, dpiece = x_ref.shape
    kpiece = g_ref.shape[1]
    brows = rows // nblk
    own = a_ref.shape[0]
    inner = 2 if ndp % 2 == 0 else 1
    outer = ndp // inner
    nx = nten // 2
    tiles, _, tile = acc.shape
    me, t = lax.axis_index("dp"), lax.axis_index("tensor")
    z, y = lax.div(me, inner), lax.rem(me, inner)
    xx, c = lax.div(t, 2), lax.rem(t, 2)

    def ten_of(rel):
        core = c if rel % 2 == 0 else 1 - c
        return 2 * lax.rem(xx + rel // 2, nx) + core

    def place_there(rel):
        return 2 * ((nx - rel // 2) % nx) + rel % 2

    barrier = pltpu.get_barrier_semaphore()

    def greet_dp(j):
        pl.semaphore_signal(
            barrier, inc=1, device_id=(lax.rem(me + j, ndp), t), device_id_type=MESH
        )

    def greet_ten(j):
        pl.semaphore_signal(
            barrier, inc=1, device_id=(me, lax.rem(t + j, nten)), device_id_type=MESH
        )

    loop(1, ndp, greet_dp)
    loop(1, nten, greet_ten)

    mine = pl.ds(me * own, own)
    local = [
        pltpu.make_async_copy(src, dst, local_sem.at[i])
        for i, (src, dst) in enumerate((
            (tok_ref, tok), (g_ref, gall.at[0]), (owner_ref, owner), (block_ref, block),
            (u_ref, uall.at[mine]), (a_ref, aall.at[mine]), (x_ref, xv),
        ))
    ]
    weights = [
        pltpu.make_async_copy(
            w_ref.at[:, pl.ds(pl.multiple_of(ten_of(rel) * kpiece, kpiece), kpiece)],
            wv.at[rel], w_sem.at[rel],
        )
        for rel in range(nten)
    ]
    for cp in local[:2] + weights[:1] + local[2:] + weights[1:]:
        cp.start()
    pl.semaphore_wait(barrier, ndp + nten - 2)

    def hop(src, way, first):
        at = pl.ds(src * own, own)
        if way == 2:
            to = inner * z + 1 - y
        else:
            to = inner * (z + 1 - 2 * way) + y
        return [
            pltpu.make_async_remote_copy(
                src_ref=(ref if first else full.at[at]),
                dst_ref=full.at[at],
                send_sem=a_send.at[i, way, src],
                recv_sem=a_recv.at[i, src],
                device_id=(to, t),
                device_id_type=MESH,
            )
            for i, (ref, full) in enumerate(((a_ref, aall), (u_ref, uall)))
        ]

    def for_ways(fn, ways):
        for way in ways:
            if way == 2:
                if inner == 2:
                    fn(2)
            else:
                ok = z + 1 < outer if way == 0 else z > 0
                pl.when(ok)(functools.partial(fn, way))

    def start_hops(src, ways, first=False):
        def go(way):
            for cp in hop(src, way, first):
                cp.start()

        for_ways(go, ways)

    def wait_hops(src, ways, first=False):
        def go(way):
            for cp in hop(src, way, first):
                cp.wait_send()

        for_ways(go, ways)

    def got_hop(src):
        for cp in hop(src, 0, False):
            cp.wait_recv()

    def line(k, fn):
        pl.when(z - k >= 0)(lambda: fn(inner * (z - k) + y, (0, 2)))
        pl.when(z + k < outer)(lambda: fn(inner * (z + k) + y, (1, 2)))

    def span_of(i):
        return pl.ds(i * brows, brows)

    def g_own(rel, i):
        there = place_there(rel)
        return pltpu.make_async_remote_copy(
            src_ref=g_ref.at[span_of(i)],
            dst_ref=gall.at[there, span_of(i)],
            send_sem=g_send.at[rel, i],
            recv_sem=g_recv.at[there, i],
            device_id=(me, ten_of(rel)),
            device_id_type=MESH,
        )

    def g_pass(j, i):
        return pltpu.make_async_remote_copy(
            src_ref=gall.at[2 * j, span_of(i)],
            dst_ref=gall.at[2 * j + 1, span_of(i)],
            send_sem=g_fwd.at[j, i],
            recv_sem=g_recv.at[2 * j + 1, i],
            device_id=(me, ten_of(1)),
            device_id_type=MESH,
        )

    def g_wait(place, i):
        pltpu.make_async_remote_copy(
            src_ref=gall.at[place, span_of(i)],
            dst_ref=gall.at[place, span_of(i)],
            send_sem=g_send.at[0, i],
            recv_sem=g_recv.at[place, i],
            device_id=(me, ten_of(1)),
            device_id_type=MESH,
        ).wait_recv()

    start_hops(me, (0, 1, 2), True)
    for i in range(nblk):
        for j in range(1, nx):
            g_own(2 * j, i).start()
    for i in range(nblk):
        g_own(1, i).start()

    local[0].wait()
    live = (tok[...] >= 0).astype(jnp.float32)
    tall = []
    for b in range(nblk):
        lane = live[:, b * brows:(b + 1) * brows]
        col = jnp.broadcast_to(lane, (brows, brows)).T.astype(jnp.bfloat16)
        reps = -(-kpiece // brows)
        tall.append(jnp.concatenate([col] * reps, axis=1)[:, :kpiece])

    def mask_piece(rel):
        for b in range(nblk):
            gm[rel, span_of(b), :] = gall[rel, span_of(b), :] * tall[b]

    def multiply(rel):
        weights[rel].wait()

        def one(n, carry):
            cols = pl.ds(pl.multiple_of(n * tile, tile), tile)
            prod = lax.dot_general(
                gm[rel], wv[rel, cols, :], LAST, preferred_element_type=jnp.float32
            )
            if rel == 0:
                acc[n] = prod
            else:
                acc[n] += prod
            return carry

        lax.fori_loop(0, tiles, one, 0)

    local[1].wait()
    mask_piece(0)
    multiply(0)

    def pass_on(src, ways):
        got_hop(src)
        start_hops(src, ways)

    def pass_g(i):
        for j in range(1, nx):
            g_wait(2 * j, i)
            g_pass(j, i).start()

    def twin_piece():
        for i in range(nblk):
            g_wait(1, i)
        mask_piece(1)
        multiply(1)

    if outer <= 4:
        for k in range(1, max(outer, nblk + 1)):
            if k < outer:
                line(k, pass_on)
            if k == 1:
                twin_piece()
            if k <= nblk:
                pass_g(k - 1)
    else:
        loop(1, outer, lambda k: line(k, pass_on))
        twin_piece()
        for i in range(nblk):
            pass_g(i)
    for j in range(1, nx):
        mask_piece(2 * j)

    for cp in local[2:]:
        cp.wait()
    slots = [owner[block[b]] for b in range(nblk)]
    if inner == 2:
        loop(0, outer, lambda k: got_hop(inner * k + 1 - y))

    def to_ten(which, rel):
        return pltpu.make_async_remote_copy(
            src_ref=part.at[which, 0], dst_ref=part.at[which, place_there(rel)],
            send_sem=p_send.at[which, rel], recv_sem=p_recv.at[which, place_there(rel)],
            device_id=(me, ten_of(rel)), device_id_type=MESH,
        )

    def from_ten(which, rel):
        pltpu.make_async_remote_copy(
            src_ref=part.at[which, 0], dst_ref=part.at[which, rel],
            send_sem=p_send.at[which, rel], recv_sem=p_recv.at[which, rel],
            device_id=(me, ten_of(rel)), device_id_type=MESH,
        ).wait_recv()

    for which, (pieces, act) in enumerate(((aall, xv), (uall, gall.at[0]))):
        for b in range(nblk):
            span = slice(b * brows, (b + 1) * brows)
            part[which, 0, :, span] = lax.dot_general(
                pieces[slots[b]], act[span, :], LAST, preferred_element_type=jnp.float32
            )
        for rel in range(nten - 1, 0, -1):
            to_ten(which, rel).start()

    for j in range(1, nx):
        multiply(2 * j)

    def summed(which):
        total = part[which, 0]
        for rel in range(1, nten):
            from_ten(which, rel)
            total = total + part[which, rel]
        return (total * live).astype(jnp.bfloat16)

    lowrank = summed(0)

    terms = []
    for b in range(nblk):
        span = slice(b * brows, (b + 1) * brows)
        terms.append(
            adapter_scale_factor
            * jnp.dot(lowrank[:, span], gm[0, span, :], preferred_element_type=jnp.float32)
        )

    def share(dev, s):
        got = jnp.zeros_like(terms[0])
        for b in range(nblk):
            got = got + jnp.where(slots[b] == dev * own + s, terms[b], 0.0)
        return got

    def to_owner(j):
        return pltpu.make_async_remote_copy(
            src_ref=gsend.at[j], dst_ref=grecv.at[j],
            send_sem=r_send.at[j], recv_sem=r_recv.at[j],
            device_id=(lax.rem(me + j, ndp), t), device_id_type=MESH,
        )

    def scatter(j):
        for s in range(own):
            gsend[j, s] = share(lax.rem(me + j, ndp), s).astype(jnp.bfloat16)
        to_owner(j).start()

    loop(1, ndp, scatter)
    for s in range(own):
        grad_ref[s] = share(me, s)

    for j in range(1, nx):
        for i in range(nblk):
            g_wait(2 * j + 1, i)
        mask_piece(2 * j + 1)
        multiply(2 * j + 1)
    hidden = summed(1) * jnp.bfloat16(adapter_scale_factor)
    outs = []
    for n in range(tiles):
        cols = slice(n * tile, (n + 1) * tile)
        for b in range(nblk):
            span = slice(b * brows, (b + 1) * brows)
            low = lax.dot_general(
                hidden[:, span], aall[slots[b], :, cols], FIRST,
                preferred_element_type=jnp.float32,
            )
            outv[n, span, :] = (acc[n, span, :] + low).astype(jnp.bfloat16)
        cp = pltpu.make_async_copy(outv.at[n], out_ref.at[:, cols], out_sem.at[n])
        cp.start()
        outs.append(cp)

    wait_hops(me, (0, 1, 2), True)
    loop(1, outer, lambda k: line(k, wait_hops))
    for i in range(nblk):
        for j in range(1, nx):
            g_own(2 * j, i).wait_send()
            g_pass(j, i).wait_send()
        g_own(1, i).wait_send()
    for which in range(2):
        for rel in range(1, nten):
            to_ten(which, rel).wait_send()

    def gather_grad(j):
        to_owner(j).wait_recv()
        grad_ref[...] += grecv[j].astype(jnp.float32)

    loop(1, ndp, gather_grad)
    loop(1, ndp, lambda j: to_owner(j).wait_send())
    for cp in outs:
        cp.wait()


def on_device(
    ndp, nten, inputs, cotangent, base_weight, down_a, up_b, block_adapter, token_adapter, owner_map
):
    rows, dpiece = inputs.shape
    kpiece = cotangent.shape[1]
    nblk = block_adapter.shape[0]
    own, rank = up_b.shape[:2]
    slots = own * ndp
    kout = base_weight.shape[1]
    nx = nten // 2
    tile = 256 if dpiece % 256 == 0 else 128
    bf16, f32 = jnp.bfloat16, jnp.float32
    hbm = pl.BlockSpec(memory_space=pltpu.HBM)
    dma = pltpu.SemaphoreType.DMA
    return pl.pallas_call(
        functools.partial(kernel, ndp, nten),
        out_shape=(
            jax.ShapeDtypeStruct((rows, dpiece), bf16),
            jax.ShapeDtypeStruct((own, rank, kpiece), f32),
        ),
        in_specs=[hbm] * 8,
        out_specs=(pl.BlockSpec(memory_space=pl.ANY), pl.BlockSpec(memory_space=pltpu.VMEM)),
        scratch_shapes=[
            pltpu.SMEM(owner_map.shape, jnp.int32),
            pltpu.SMEM((nblk,), jnp.int32),
            pltpu.VMEM((1, rows), jnp.int32),
            pltpu.VMEM((rows, dpiece), bf16),
            pltpu.VMEM((nten, dpiece, kpiece), bf16),
            pltpu.VMEM((nten, rows, kpiece), bf16),
            pltpu.VMEM((nten, rows, kpiece), bf16),
            pltpu.VMEM((dpiece // tile, rows, tile), f32),
            pltpu.VMEM((slots, rank, dpiece), bf16),
            pltpu.VMEM((slots, rank, kpiece), bf16),
            pltpu.VMEM((2, nten, rank, rows), f32),
            pltpu.VMEM((dpiece // tile, rows, tile), bf16),
            pltpu.VMEM((ndp, own, rank, kpiece), bf16),
            pltpu.VMEM((ndp, own, rank, kpiece), bf16),
            dma((7,)),
            dma((nten,)),
            dma((dpiece // tile,)),
            dma((2, 3, ndp)),
            dma((2, ndp)),
            dma((nten, nblk)),
            dma((nx, nblk)),
            dma((nten, nblk)),
            dma((2, nten)),
            dma((2, nten)),
            dma((ndp,)),
            dma((ndp,)),
        ],
        cost_estimate=pl.CostEstimate(
            flops=2 * rows * dpiece * (kout + 2 * rank),
            bytes_accessed=2 * (2 * rows * dpiece + dpiece * kout + rows * kpiece),
            transcendentals=0,
        ),
        compiler_params=pltpu.CompilerParams(
            collective_id=0, has_side_effects=True, vmem_limit_bytes=64 * 2**20 - 2**18
        ),
    )(
        owner_map, block_adapter, token_adapter.reshape(1, rows), inputs, cotangent, base_weight,
        jnp.swapaxes(down_a, 1, 2), up_b,
    )


def solution(mesh):
    in_specs = (
        P("dp", "tensor"),
        P("dp", "tensor"),
        P("tensor", None),
        P("dp", "tensor", None),
        P("dp", None, "tensor"),
        P("dp"),
        P("dp"),
        P(),
    )
    out_specs = (P("dp", "tensor"), P("dp", None, "tensor"))
    return jax.shard_map(
        functools.partial(on_device, mesh.shape["dp"], mesh.shape["tensor"]),
        mesh=mesh, in_specs=in_specs, out_specs=out_specs, check_vma=False,
    )
```

```python
import functools

import jax
import jax.numpy as jnp
from jax import lax
from jax.experimental import pallas as pl
from jax.experimental.pallas import tpu as pltpu
from jax.sharding import PartitionSpec as P

adapter_scale_factor = 2.0
MESH = pl.DeviceIdType.MESH
LAST = (((1,), (1,)), ((), ()))
FIRST = (((0,), (0,)), ((), ()))


def loop(lo, hi, body):
    if hi - lo <= 8:
        for i in range(lo, hi):
            body(i)
    else:
        lax.fori_loop(lo, hi, lambda i, c: (body(i), c)[1], 0)


def kernel(
    ndp, nten, owner_ref, block_ref, tok_ref, x_ref, g_ref, w_ref, a_ref, u_ref,
    out_ref, grad_ref,
    owner, block, tok, xv, wv, gall, gm, acc, aall, uall, part, outv, gsend, grecv,
    local_sem, w_sem, out_sem, a_send, a_recv, u_send, u_recv, g_send, g_fwd, g_recv,
    p_send, p_recv, r_send, r_recv,
):
    nblk = block_ref.shape[0]
    rows, dpiece = x_ref.shape
    kpiece = g_ref.shape[1]
    brows = rows // nblk
    own = a_ref.shape[0]
    inner = 2 if ndp % 2 == 0 else 1
    outer = ndp // inner
    nx = nten // 2
    tiles, _, tile = acc.shape
    me, t = lax.axis_index("dp"), lax.axis_index("tensor")
    z, y = lax.div(me, inner), lax.rem(me, inner)
    xx, c = lax.div(t, 2), lax.rem(t, 2)

    def ten_of(rel):
        core = c if rel % 2 == 0 else 1 - c
        return 2 * lax.rem(xx + rel // 2, nx) + core

    def place_there(rel):
        return 2 * ((nx - rel // 2) % nx) + rel % 2

    barrier = pltpu.get_barrier_semaphore()

    def greet_dp(j):
        pl.semaphore_signal(
            barrier, inc=1, device_id=(lax.rem(me + j, ndp), t), device_id_type=MESH
        )

    def greet_ten(j):
        pl.semaphore_signal(
            barrier, inc=1, device_id=(me, lax.rem(t + j, nten)), device_id_type=MESH
        )

    loop(1, ndp, greet_dp)
    loop(1, nten, greet_ten)

    mine = pl.ds(me * own, own)
    local = [
        pltpu.make_async_copy(src, dst, local_sem.at[i])
        for i, (src, dst) in enumerate((
            (tok_ref, tok), (g_ref, gall.at[0]), (owner_ref, owner), (block_ref, block),
            (u_ref, uall.at[mine]), (a_ref, aall.at[mine]), (x_ref, xv),
        ))
    ]
    weights = [
        pltpu.make_async_copy(
            w_ref.at[:, pl.ds(pl.multiple_of(ten_of(rel) * kpiece, kpiece), kpiece)],
            wv.at[rel], w_sem.at[rel],
        )
        for rel in range(nten)
    ]
    for cp in local[:2] + weights[:1] + local[2:] + weights[1:]:
        cp.start()
    pl.semaphore_wait(barrier, ndp + nten - 2)

    def hop(src, k, way, first):
        slot = src * own + k
        if way == 2:
            to = inner * z + 1 - y
        else:
            to = inner * (z + 1 - 2 * way) + y
        return pltpu.make_async_remote_copy(
            src_ref=(a_ref.at[k] if first else aall.at[slot]),
            dst_ref=aall.at[slot],
            send_sem=a_send.at[way, slot],
            recv_sem=a_recv.at[slot],
            device_id=(to, t),
            device_id_type=MESH,
        )

    def to_peer(j):
        return pltpu.make_async_remote_copy(
            src_ref=u_ref,
            dst_ref=uall.at[mine],
            send_sem=u_send.at[j],
            recv_sem=u_recv.at[j],
            device_id=(lax.rem(me + j, ndp), t),
            device_id_type=MESH,
        )

    def from_peer(j):
        at = pl.ds(lax.rem(me + ndp - j, ndp) * own, own)
        pltpu.make_async_remote_copy(
            src_ref=u_ref,
            dst_ref=uall.at[at],
            send_sem=u_send.at[j],
            recv_sem=u_recv.at[j],
            device_id=(lax.rem(me + j, ndp), t),
            device_id_type=MESH,
        ).wait_recv()

    def for_ways(fn, ways):
        for way in ways:
            if way == 2:
                if inner == 2:
                    fn(2)
            else:
                ok = z + 1 < outer if way == 0 else z > 0
                pl.when(ok)(functools.partial(fn, way))

    def start_hops(src, k, ways, first=False):
        for_ways(lambda way: hop(src, k, way, first).start(), ways)

    def wait_hops(src, k, ways, first=False):
        for_ways(lambda way: hop(src, k, way, first).wait_send(), ways)

    def got_hop(src, k):
        hop(src, k, 0, False).wait_recv()

    def line(d, k, fn):
        pl.when(z - d >= 0)(lambda: fn(inner * (z - d) + y, k, (0, 2)))
        pl.when(z + d < outer)(lambda: fn(inner * (z + d) + y, k, (1, 2)))

    def lines(d, fn):
        for k in range(own):
            line(d, k, fn)

    def span_of(i):
        return pl.ds(i * brows, brows)

    def g_own(rel, i):
        there = place_there(rel)
        return pltpu.make_async_remote_copy(
            src_ref=g_ref.at[span_of(i)],
            dst_ref=gall.at[there, span_of(i)],
            send_sem=g_send.at[rel, i],
            recv_sem=g_recv.at[there, i],
            device_id=(me, ten_of(rel)),
            device_id_type=MESH,
        )

    def g_pass(j, i):
        return pltpu.make_async_remote_copy(
            src_ref=gall.at[2 * j, span_of(i)],
            dst_ref=gall.at[2 * j + 1, span_of(i)],
            send_sem=g_fwd.at[j, i],
            recv_sem=g_recv.at[2 * j + 1, i],
            device_id=(me, ten_of(1)),
            device_id_type=MESH,
        )

    def g_wait(place, i):
        pltpu.make_async_remote_copy(
            src_ref=gall.at[place, span_of(i)],
            dst_ref=gall.at[place, span_of(i)],
            send_sem=g_send.at[0, i],
            recv_sem=g_recv.at[place, i],
            device_id=(me, ten_of(1)),
            device_id_type=MESH,
        ).wait_recv()

    for k in range(own):
        start_hops(me, k, (0, 1, 2), True)
    for i in range(nblk):
        for j in range(1, nx):
            g_own(2 * j, i).start()
    for i in range(nblk):
        g_own(1, i).start()

    local[0].wait()
    live = (tok[...] >= 0).astype(jnp.float32)
    tall = []
    for b in range(nblk):
        lane = live[:, b * brows:(b + 1) * brows]
        col = jnp.broadcast_to(lane, (brows, brows)).T.astype(jnp.bfloat16)
        reps = -(-kpiece // brows)
        tall.append(jnp.concatenate([col] * reps, axis=1)[:, :kpiece])

    def mask_piece(rel):
        for b in range(nblk):
            gm[rel, span_of(b), :] = gall[rel, span_of(b), :] * tall[b]

    def multiply(rel):
        weights[rel].wait()

        def one(n, carry):
            cols = pl.ds(pl.multiple_of(n * tile, tile), tile)
            prod = lax.dot_general(
                gm[rel], wv[rel, cols, :], LAST, preferred_element_type=jnp.float32
            )
            if rel == 0:
                acc[n] = prod
            else:
                acc[n] += prod
            return carry

        lax.fori_loop(0, tiles, one, 0)

    local[1].wait()
    mask_piece(0)
    multiply(0)

    def pass_on(src, k, ways):
        got_hop(src, k)
        start_hops(src, k, ways)

    def pass_g(i):
        for j in range(1, nx):
            g_wait(2 * j, i)
            g_pass(j, i).start()

    def twin_piece():
        for i in range(nblk):
            g_wait(1, i)
        mask_piece(1)
        multiply(1)

    if outer <= 4:
        for k in range(1, max(outer, nblk + 1)):
            if k < outer:
                lines(k, pass_on)
            if k == 1:
                twin_piece()
            if k <= nblk:
                pass_g(k - 1)
    else:
        loop(1, outer, lambda d: lines(d, pass_on))
        twin_piece()
        for i in range(nblk):
            pass_g(i)
    loop(1, ndp, lambda j: to_peer(j).start())
    for j in range(1, nx):
        mask_piece(2 * j)

    for cp in local[2:]:
        cp.wait()
    slots = [owner[block[b]] for b in range(nblk)]
    if inner == 2:
        for k in range(own):
            loop(0, outer, lambda d: got_hop(inner * d + 1 - y, k))

    def to_ten(which, rel):
        return pltpu.make_async_remote_copy(
            src_ref=part.at[which, 0], dst_ref=part.at[which, place_there(rel)],
            send_sem=p_send.at[which, rel], recv_sem=p_recv.at[which, place_there(rel)],
            device_id=(me, ten_of(rel)), device_id_type=MESH,
        )

    def from_ten(which, rel):
        pltpu.make_async_remote_copy(
            src_ref=part.at[which, 0], dst_ref=part.at[which, rel],
            send_sem=p_send.at[which, rel], recv_sem=p_recv.at[which, rel],
            device_id=(me, ten_of(rel)), device_id_type=MESH,
        ).wait_recv()

    for which, (pieces, act) in enumerate(((aall, xv), (uall, gall.at[0]))):
        if which == 1:
            loop(1, ndp, from_peer)
        for b in range(nblk):
            span = slice(b * brows, (b + 1) * brows)
            part[which, 0, :, span] = lax.dot_general(
                pieces[slots[b]], act[span, :], LAST, preferred_element_type=jnp.float32
            )
        for rel in range(nten - 1, 0, -1):
            to_ten(which, rel).start()

    for j in range(1, nx):
        multiply(2 * j)

    def summed(which):
        total = part[which, 0]
        for rel in range(1, nten):
            from_ten(which, rel)
            total = total + part[which, rel]
        return (total * live).astype(jnp.bfloat16)

    lowrank = summed(0)

    terms = []
    for b in range(nblk):
        span = slice(b * brows, (b + 1) * brows)
        terms.append(
            adapter_scale_factor
            * jnp.dot(lowrank[:, span], gm[0, span, :], preferred_element_type=jnp.float32)
        )

    def share(dev, s):
        got = jnp.zeros_like(terms[0])
        for b in range(nblk):
            got = got + jnp.where(slots[b] == dev * own + s, terms[b], 0.0)
        return got

    def to_owner(j):
        return pltpu.make_async_remote_copy(
            src_ref=gsend.at[j], dst_ref=grecv.at[j],
            send_sem=r_send.at[j], recv_sem=r_recv.at[j],
            device_id=(lax.rem(me + j, ndp), t), device_id_type=MESH,
        )

    def scatter(j):
        for s in range(own):
            gsend[j, s] = share(lax.rem(me + j, ndp), s).astype(jnp.bfloat16)
        to_owner(j).start()

    loop(1, ndp, scatter)
    for s in range(own):
        grad_ref[s] = share(me, s)

    for j in range(1, nx):
        for i in range(nblk):
            g_wait(2 * j + 1, i)
        mask_piece(2 * j + 1)
        multiply(2 * j + 1)
    hidden = summed(1) * jnp.bfloat16(adapter_scale_factor)
    outs = []
    for n in range(tiles):
        cols = slice(n * tile, (n + 1) * tile)
        for b in range(nblk):
            span = slice(b * brows, (b + 1) * brows)
            low = lax.dot_general(
                hidden[:, span], aall[slots[b], :, cols], FIRST,
                preferred_element_type=jnp.float32,
            )
            outv[n, span, :] = (acc[n, span, :] + low).astype(jnp.bfloat16)
        cp = pltpu.make_async_copy(outv.at[n], out_ref.at[:, cols], out_sem.at[n])
        cp.start()
        outs.append(cp)

    for k in range(own):
        wait_hops(me, k, (0, 1, 2), True)
    loop(1, outer, lambda d: lines(d, wait_hops))
    loop(1, ndp, lambda j: to_peer(j).wait_send())
    for i in range(nblk):
        for j in range(1, nx):
            g_own(2 * j, i).wait_send()
            g_pass(j, i).wait_send()
        g_own(1, i).wait_send()
    for which in range(2):
        for rel in range(1, nten):
            to_ten(which, rel).wait_send()

    def gather_grad(j):
        to_owner(j).wait_recv()
        grad_ref[...] += grecv[j].astype(jnp.float32)

    loop(1, ndp, gather_grad)
    loop(1, ndp, lambda j: to_owner(j).wait_send())
    for cp in outs:
        cp.wait()


def hand_over(out_ref, grad_ref, out_to, grad_to, sem):
    parts = sem.shape[0] - 1
    rows = out_ref.shape[0] // parts
    copies = [pltpu.make_async_copy(grad_ref, grad_to, sem.at[parts])]
    for i in range(parts):
        at = pl.ds(i * rows, rows)
        copies.append(pltpu.make_async_copy(out_ref.at[at], out_to.at[at], sem.at[i]))
    for cp in copies:
        cp.start()
    for cp in copies:
        cp.wait()


def on_device(
    ndp, nten, inputs, cotangent, base_weight, down_a, up_b, block_adapter, token_adapter, owner_map
):
    rows, dpiece = inputs.shape
    kpiece = cotangent.shape[1]
    nblk = block_adapter.shape[0]
    own, rank = up_b.shape[:2]
    slots = own * ndp
    kout = base_weight.shape[1]
    nx = nten // 2
    tile = 256 if dpiece % 256 == 0 else 128
    bf16, f32 = jnp.bfloat16, jnp.float32
    hbm = pl.BlockSpec(memory_space=pltpu.HBM)
    dma = pltpu.SemaphoreType.DMA
    results = pl.pallas_call(
        functools.partial(kernel, ndp, nten),
        out_shape=(
            jax.ShapeDtypeStruct((rows, dpiece), bf16),
            jax.ShapeDtypeStruct((own, rank, kpiece), f32),
        ),
        in_specs=[hbm] * 8,
        out_specs=(pl.BlockSpec(memory_space=pl.ANY), pl.BlockSpec(memory_space=pltpu.VMEM)),
        scratch_shapes=[
            pltpu.SMEM(owner_map.shape, jnp.int32),
            pltpu.SMEM((nblk,), jnp.int32),
            pltpu.VMEM((1, rows), jnp.int32),
            pltpu.VMEM((rows, dpiece), bf16),
            pltpu.VMEM((nten, dpiece, kpiece), bf16),
            pltpu.VMEM((nten, rows, kpiece), bf16),
            pltpu.VMEM((nten, rows, kpiece), bf16),
            pltpu.VMEM((dpiece // tile, rows, tile), f32),
            pltpu.VMEM((slots, rank, dpiece), bf16),
            pltpu.VMEM((slots, rank, kpiece), bf16),
            pltpu.VMEM((2, nten, rank, rows), f32),
            pltpu.VMEM((dpiece // tile, rows, tile), bf16),
            pltpu.VMEM((ndp, own, rank, kpiece), bf16),
            pltpu.VMEM((ndp, own, rank, kpiece), bf16),
            dma((7,)),
            dma((nten,)),
            dma((dpiece // tile,)),
            dma((3, slots)),
            dma((slots,)),
            dma((ndp,)),
            dma((ndp,)),
            dma((nten, nblk)),
            dma((nx, nblk)),
            dma((nten, nblk)),
            dma((2, nten)),
            dma((2, nten)),
            dma((ndp,)),
            dma((ndp,)),
        ],
        cost_estimate=pl.CostEstimate(
            flops=2 * rows * dpiece * (kout + 2 * rank),
            bytes_accessed=2 * (2 * rows * dpiece + dpiece * kout + rows * kpiece),
            transcendentals=0,
        ),
        compiler_params=pltpu.CompilerParams(
            collective_id=0, has_side_effects=True, vmem_limit_bytes=64 * 2**20 - 2**18
        ),
    )(
        owner_map, block_adapter, token_adapter.reshape(1, rows), inputs, cotangent, base_weight,
        jnp.swapaxes(down_a, 1, 2), up_b,
    )
    return pl.pallas_call(
        hand_over,
        out_shape=tuple(jax.ShapeDtypeStruct(r.shape, r.dtype) for r in results),
        in_specs=[hbm] * 2,
        out_specs=(hbm, hbm),
        scratch_shapes=[dma((nblk + 1,))],
        cost_estimate=pl.CostEstimate(
            flops=0, bytes_accessed=4 * rows * dpiece, transcendentals=0
        ),
        compiler_params=pltpu.CompilerParams(vmem_limit_bytes=64 * 2**20 - 2**18),
    )(*results)


def solution(mesh):
    in_specs = (
        P("dp", "tensor"),
        P("dp", "tensor"),
        P("tensor", None),
        P("dp", "tensor", None),
        P("dp", None, "tensor"),
        P("dp"),
        P("dp"),
        P(),
    )
    out_specs = (P("dp", "tensor"), P("dp", None, "tensor"))
    return jax.shard_map(
        functools.partial(on_device, mesh.shape["dp"], mesh.shape["tensor"]),
        mesh=mesh, in_specs=in_specs, out_specs=out_specs, check_vma=False,
    )
```

```python
import functools

import jax
import jax.numpy as jnp
from jax import lax
from jax.experimental import pallas as pl
from jax.experimental.pallas import tpu as pltpu
from jax.sharding import PartitionSpec as P

adapter_scale_factor = 2.0
MESH = pl.DeviceIdType.MESH
LAST = (((1,), (1,)), ((), ()))
FIRST = (((0,), (0,)), ((), ()))


def loop(lo, hi, body):
    if hi - lo <= 8:
        for i in range(lo, hi):
            body(i)
    else:
        lax.fori_loop(lo, hi, lambda i, c: (body(i), c)[1], 0)


def kernel(
    ndp, nten, owner_ref, block_ref, tok_ref, x_ref, g_ref, w_ref, a_ref, u_ref,
    out_ref, grad_ref,
    owner, block, tok, xv, wv, gall, gm, acc, aall, uall, part, outv, gsend, grecv,
    local_sem, w_sem, out_sem, a_send, a_recv, u_send, u_recv, g_send, g_fwd, g_recv,
    p_send, p_recv, r_send, r_recv,
):
    nblk = block_ref.shape[0]
    rows, dpiece = x_ref.shape
    kpiece = g_ref.shape[1]
    brows = rows // nblk
    own = a_ref.shape[0]
    inner = 2 if ndp % 2 == 0 else 1
    outer = ndp // inner
    nx = nten // 2
    tiles, _, tile = acc.shape
    me, t = lax.axis_index("dp"), lax.axis_index("tensor")
    z, y = lax.div(me, inner), lax.rem(me, inner)
    xx, c = lax.div(t, 2), lax.rem(t, 2)

    def ten_of(rel):
        core = c if rel % 2 == 0 else 1 - c
        return 2 * lax.rem(xx + rel // 2, nx) + core

    def place_there(rel):
        return 2 * ((nx - rel // 2) % nx) + rel % 2

    barrier = pltpu.get_barrier_semaphore()

    def greet_dp(j):
        pl.semaphore_signal(
            barrier, inc=1, device_id=(lax.rem(me + j, ndp), t), device_id_type=MESH
        )

    def greet_ten(j):
        pl.semaphore_signal(
            barrier, inc=1, device_id=(me, lax.rem(t + j, nten)), device_id_type=MESH
        )

    loop(1, ndp, greet_dp)
    loop(1, nten, greet_ten)

    mine = pl.ds(me * own, own)
    local = [
        pltpu.make_async_copy(src, dst, local_sem.at[i])
        for i, (src, dst) in enumerate((
            (tok_ref, tok), (g_ref, gall.at[0]), (owner_ref, owner), (block_ref, block),
            (u_ref, uall.at[mine]), (a_ref, aall.at[mine]), (x_ref, xv),
        ))
    ]
    weights = [
        pltpu.make_async_copy(
            w_ref.at[:, pl.ds(pl.multiple_of(ten_of(rel) * kpiece, kpiece), kpiece)],
            wv.at[rel], w_sem.at[rel],
        )
        for rel in range(nten)
    ]
    for cp in local[:2] + weights[:1] + local[2:] + weights[1:]:
        cp.start()
    pl.semaphore_wait(barrier, ndp + nten - 2)

    def hop(src, k, way, first):
        slot = src * own + k
        if way == 2:
            to = inner * z + 1 - y
        else:
            to = inner * (z + 1 - 2 * way) + y
        return pltpu.make_async_remote_copy(
            src_ref=(a_ref.at[k] if first else aall.at[slot]),
            dst_ref=aall.at[slot],
            send_sem=a_send.at[way, slot],
            recv_sem=a_recv.at[slot],
            device_id=(to, t),
            device_id_type=MESH,
        )

    def to_peer(j):
        return pltpu.make_async_remote_copy(
            src_ref=u_ref,
            dst_ref=uall.at[mine],
            send_sem=u_send.at[j],
            recv_sem=u_recv.at[j],
            device_id=(lax.rem(me + j, ndp), t),
            device_id_type=MESH,
        )

    def from_peer(j):
        at = pl.ds(lax.rem(me + ndp - j, ndp) * own, own)
        pltpu.make_async_remote_copy(
            src_ref=u_ref,
            dst_ref=uall.at[at],
            send_sem=u_send.at[j],
            recv_sem=u_recv.at[j],
            device_id=(lax.rem(me + j, ndp), t),
            device_id_type=MESH,
        ).wait_recv()

    def for_ways(fn, ways):
        for way in ways:
            if way == 2:
                if inner == 2:
                    fn(2)
            else:
                ok = z + 1 < outer if way == 0 else z > 0
                pl.when(ok)(functools.partial(fn, way))

    def start_hops(src, k, ways, first=False):
        for_ways(lambda way: hop(src, k, way, first).start(), ways)

    def wait_hops(src, k, ways, first=False):
        for_ways(lambda way: hop(src, k, way, first).wait_send(), ways)

    def got_hop(src, k):
        hop(src, k, 0, False).wait_recv()

    def line(d, k, fn):
        pl.when(z - d >= 0)(lambda: fn(inner * (z - d) + y, k, (0, 2)))
        pl.when(z + d < outer)(lambda: fn(inner * (z + d) + y, k, (1, 2)))

    def lines(d, fn):
        for k in range(own):
            line(d, k, fn)

    def span_of(i):
        return pl.ds(i * brows, brows)

    def g_own(rel, i):
        there = place_there(rel)
        return pltpu.make_async_remote_copy(
            src_ref=g_ref.at[span_of(i)],
            dst_ref=gall.at[there, span_of(i)],
            send_sem=g_send.at[rel, i],
            recv_sem=g_recv.at[there, i],
            device_id=(me, ten_of(rel)),
            device_id_type=MESH,
        )

    def g_pass(j, i):
        return pltpu.make_async_remote_copy(
            src_ref=gall.at[2 * j, span_of(i)],
            dst_ref=gall.at[2 * j + 1, span_of(i)],
            send_sem=g_fwd.at[j, i],
            recv_sem=g_recv.at[2 * j + 1, i],
            device_id=(me, ten_of(1)),
            device_id_type=MESH,
        )

    def g_wait(place, i):
        pltpu.make_async_remote_copy(
            src_ref=gall.at[place, span_of(i)],
            dst_ref=gall.at[place, span_of(i)],
            send_sem=g_send.at[0, i],
            recv_sem=g_recv.at[place, i],
            device_id=(me, ten_of(1)),
            device_id_type=MESH,
        ).wait_recv()

    for k in range(own):
        start_hops(me, k, (0, 1, 2), True)
    for i in range(nblk):
        for j in range(1, nx):
            g_own(2 * j, i).start()
    for i in range(nblk):
        g_own(1, i).start()

    local[0].wait()
    live = (tok[...] >= 0).astype(jnp.float32)
    tall = []
    for b in range(nblk):
        lane = live[:, b * brows:(b + 1) * brows]
        col = jnp.broadcast_to(lane, (brows, brows)).T.astype(jnp.bfloat16)
        reps = -(-kpiece // brows)
        tall.append(jnp.concatenate([col] * reps, axis=1)[:, :kpiece])

    def mask_piece(rel):
        for b in range(nblk):
            gm[rel, span_of(b), :] = gall[rel, span_of(b), :] * tall[b]

    def multiply(rel):
        weights[rel].wait()

        def one(n, carry):
            cols = pl.ds(pl.multiple_of(n * tile, tile), tile)
            prod = lax.dot_general(
                gm[rel], wv[rel, cols, :], LAST, preferred_element_type=jnp.float32
            )
            if rel == 0:
                acc[n] = prod
            else:
                acc[n] += prod
            return carry

        lax.fori_loop(0, tiles, one, 0)

    local[1].wait()
    mask_piece(0)

    def pass_on(src, k, ways):
        got_hop(src, k)
        start_hops(src, k, ways)

    def pass_g(i):
        for j in range(1, nx):
            g_wait(2 * j, i)
            g_pass(j, i).start()

    def twin_piece():
        for i in range(nblk):
            g_wait(1, i)
        mask_piece(1)
        multiply(1)

    if outer <= 4:
        for k in range(1, max(outer, nblk + 1)):
            if k < outer:
                lines(k, pass_on)
            if k <= nblk:
                pass_g(k - 1)
            if k == 1:
                multiply(0)
            if k == 2:
                twin_piece()
    else:
        loop(1, outer, lambda d: lines(d, pass_on))
        multiply(0)
        twin_piece()
        for i in range(nblk):
            pass_g(i)
    loop(1, ndp, lambda j: to_peer(j).start())
    for j in range(1, nx):
        mask_piece(2 * j)
        multiply(2 * j)

    for cp in local[2:]:
        cp.wait()
    slots = [owner[block[b]] for b in range(nblk)]
    if inner == 2:
        for k in range(own):
            loop(0, outer, lambda d: got_hop(inner * d + 1 - y, k))

    def to_ten(which, rel):
        return pltpu.make_async_remote_copy(
            src_ref=part.at[which, 0], dst_ref=part.at[which, place_there(rel)],
            send_sem=p_send.at[which, rel], recv_sem=p_recv.at[which, place_there(rel)],
            device_id=(me, ten_of(rel)), device_id_type=MESH,
        )

    def from_ten(which, rel):
        pltpu.make_async_remote_copy(
            src_ref=part.at[which, 0], dst_ref=part.at[which, rel],
            send_sem=p_send.at[which, rel], recv_sem=p_recv.at[which, rel],
            device_id=(me, ten_of(rel)), device_id_type=MESH,
        ).wait_recv()

    for which, (pieces, act) in enumerate(((aall, xv), (uall, gall.at[0]))):
        if which == 1:
            loop(1, ndp, from_peer)
        for b in range(nblk):
            span = slice(b * brows, (b + 1) * brows)
            part[which, 0, :, span] = lax.dot_general(
                pieces[slots[b]], act[span, :], LAST, preferred_element_type=jnp.float32
            )
        for rel in range(nten - 1, 0, -1):
            to_ten(which, rel).start()

    for j in range(1, nx):
        for i in range(nblk):
            g_wait(2 * j + 1, i)
        mask_piece(2 * j + 1)
        multiply(2 * j + 1)

    def summed(which):
        total = part[which, 0]
        for rel in range(1, nten):
            from_ten(which, rel)
            total = total + part[which, rel]
        return (total * live).astype(jnp.bfloat16)

    lowrank = summed(0)

    terms = []
    for b in range(nblk):
        span = slice(b * brows, (b + 1) * brows)
        terms.append(
            adapter_scale_factor
            * jnp.dot(lowrank[:, span], gm[0, span, :], preferred_element_type=jnp.float32)
        )

    def share(dev, s):
        got = jnp.zeros_like(terms[0])
        for b in range(nblk):
            got = got + jnp.where(slots[b] == dev * own + s, terms[b], 0.0)
        return got

    def to_owner(j):
        return pltpu.make_async_remote_copy(
            src_ref=gsend.at[j], dst_ref=grecv.at[j],
            send_sem=r_send.at[j], recv_sem=r_recv.at[j],
            device_id=(lax.rem(me + j, ndp), t), device_id_type=MESH,
        )

    def scatter(j):
        for s in range(own):
            gsend[j, s] = share(lax.rem(me + j, ndp), s).astype(jnp.bfloat16)
        to_owner(j).start()

    loop(1, ndp, scatter)
    for s in range(own):
        grad_ref[s] = share(me, s)

    hidden = summed(1) * jnp.bfloat16(adapter_scale_factor)
    outs = []
    for n in range(tiles):
        cols = slice(n * tile, (n + 1) * tile)
        for b in range(nblk):
            span = slice(b * brows, (b + 1) * brows)
            low = lax.dot_general(
                hidden[:, span], aall[slots[b], :, cols], FIRST,
                preferred_element_type=jnp.float32,
            )
            outv[n, span, :] = (acc[n, span, :] + low).astype(jnp.bfloat16)
        cp = pltpu.make_async_copy(outv.at[n], out_ref.at[:, cols], out_sem.at[n])
        cp.start()
        outs.append(cp)

    for k in range(own):
        wait_hops(me, k, (0, 1, 2), True)
    loop(1, outer, lambda d: lines(d, wait_hops))
    loop(1, ndp, lambda j: to_peer(j).wait_send())
    for i in range(nblk):
        for j in range(1, nx):
            g_own(2 * j, i).wait_send()
            g_pass(j, i).wait_send()
        g_own(1, i).wait_send()
    for which in range(2):
        for rel in range(1, nten):
            to_ten(which, rel).wait_send()

    def gather_grad(j):
        to_owner(j).wait_recv()
        grad_ref[...] += grecv[j].astype(jnp.float32)

    loop(1, ndp, gather_grad)
    loop(1, ndp, lambda j: to_owner(j).wait_send())
    for cp in outs:
        cp.wait()


def hand_over(out_ref, grad_ref, out_to, grad_to, out_held, grad_held, sem_in, sem_out):
    parts = sem_in.shape[0] - 1
    rows = out_ref.shape[0] // parts
    ways = [(grad_ref, grad_held, grad_to)]
    for i in range(parts):
        at = pl.ds(i * rows, rows)
        ways.append((out_ref.at[at], out_held.at[at], out_to.at[at]))
    ins = [pltpu.make_async_copy(a, b, sem_in.at[i]) for i, (a, b, _) in enumerate(ways)]
    outs = [pltpu.make_async_copy(b, c, sem_out.at[i]) for i, (_, b, c) in enumerate(ways)]
    for cp in ins:
        cp.start()
    for cp, then in zip(ins, outs):
        cp.wait()
        then.start()
    for cp in outs:
        cp.wait()


def on_device(
    ndp, nten, inputs, cotangent, base_weight, down_a, up_b, block_adapter, token_adapter, owner_map
):
    rows, dpiece = inputs.shape
    kpiece = cotangent.shape[1]
    nblk = block_adapter.shape[0]
    own, rank = up_b.shape[:2]
    slots = own * ndp
    kout = base_weight.shape[1]
    nx = nten // 2
    tile = 256 if dpiece % 256 == 0 else 128
    bf16, f32 = jnp.bfloat16, jnp.float32
    hbm = pl.BlockSpec(memory_space=pltpu.HBM)
    dma = pltpu.SemaphoreType.DMA
    results = pl.pallas_call(
        functools.partial(kernel, ndp, nten),
        out_shape=(
            jax.ShapeDtypeStruct((rows, dpiece), bf16),
            jax.ShapeDtypeStruct((own, rank, kpiece), f32),
        ),
        in_specs=[hbm] * 8,
        out_specs=(pl.BlockSpec(memory_space=pl.ANY), pl.BlockSpec(memory_space=pltpu.VMEM)),
        scratch_shapes=[
            pltpu.SMEM(owner_map.shape, jnp.int32),
            pltpu.SMEM((nblk,), jnp.int32),
            pltpu.VMEM((1, rows), jnp.int32),
            pltpu.VMEM((rows, dpiece), bf16),
            pltpu.VMEM((nten, dpiece, kpiece), bf16),
            pltpu.VMEM((nten, rows, kpiece), bf16),
            pltpu.VMEM((nten, rows, kpiece), bf16),
            pltpu.VMEM((dpiece // tile, rows, tile), f32),
            pltpu.VMEM((slots, rank, dpiece), bf16),
            pltpu.VMEM((slots, rank, kpiece), bf16),
            pltpu.VMEM((2, nten, rank, rows), f32),
            pltpu.VMEM((dpiece // tile, rows, tile), bf16),
            pltpu.VMEM((ndp, own, rank, kpiece), bf16),
            pltpu.VMEM((ndp, own, rank, kpiece), bf16),
            dma((7,)),
            dma((nten,)),
            dma((dpiece // tile,)),
            dma((3, slots)),
            dma((slots,)),
            dma((ndp,)),
            dma((ndp,)),
            dma((nten, nblk)),
            dma((nx, nblk)),
            dma((nten, nblk)),
            dma((2, nten)),
            dma((2, nten)),
            dma((ndp,)),
            dma((ndp,)),
        ],
        cost_estimate=pl.CostEstimate(
            flops=2 * rows * dpiece * (kout + 2 * rank),
            bytes_accessed=2 * (2 * rows * dpiece + dpiece * kout + rows * kpiece),
            transcendentals=0,
        ),
        compiler_params=pltpu.CompilerParams(
            collective_id=0, has_side_effects=True, vmem_limit_bytes=64 * 2**20 - 2**18
        ),
    )(
        owner_map, block_adapter, token_adapter.reshape(1, rows), inputs, cotangent, base_weight,
        jnp.swapaxes(down_a, 1, 2), up_b,
    )
    return pl.pallas_call(
        hand_over,
        out_shape=tuple(jax.ShapeDtypeStruct(r.shape, r.dtype) for r in results),
        in_specs=[hbm] * 2,
        out_specs=(hbm, hbm),
        scratch_shapes=[
            pltpu.VMEM((rows, dpiece), bf16),
            pltpu.VMEM((own, rank, kpiece), f32),
            dma((nblk + 1,)),
            dma((nblk + 1,)),
        ],
        cost_estimate=pl.CostEstimate(
            flops=0, bytes_accessed=4 * rows * dpiece, transcendentals=0
        ),
        compiler_params=pltpu.CompilerParams(vmem_limit_bytes=64 * 2**20 - 2**18),
    )(*results)


def solution(mesh):
    in_specs = (
        P("dp", "tensor"),
        P("dp", "tensor"),
        P("tensor", None),
        P("dp", "tensor", None),
        P("dp", None, "tensor"),
        P("dp"),
        P("dp"),
        P(),
    )
    out_specs = (P("dp", "tensor"), P("dp", None, "tensor"))
    return jax.shard_map(
        functools.partial(on_device, mesh.shape["dp"], mesh.shape["tensor"]),
        mesh=mesh, in_specs=in_specs, out_specs=out_specs, check_vma=False,
    )
```

```python
import functools

import jax
import jax.numpy as jnp
from jax import lax
from jax.experimental import pallas as pl
from jax.experimental.pallas import tpu as pltpu
from jax.sharding import PartitionSpec as P

adapter_scale_factor = 2.0
MESH = pl.DeviceIdType.MESH
LAST = (((1,), (1,)), ((), ()))
FIRST = (((0,), (0,)), ((), ()))


def loop(lo, hi, body):
    if hi - lo <= 8:
        for i in range(lo, hi):
            body(i)
    else:
        lax.fori_loop(lo, hi, lambda i, c: (body(i), c)[1], 0)


def kernel(
    ndp, nten, owner_ref, block_ref, tok_ref, x_ref, g_ref, w_ref, a_ref, u_ref,
    out_ref, grad_ref,
    owner, block, tok, xv, wv, gall, gm, acc, aall, uall, part, outv, gsend, grecv,
    local_sem, w_sem, out_sem, a_send, a_recv, u_send, u_recv, g_send, g_fwd, g_recv,
    p_send, p_recv, r_send, r_recv,
):
    nblk = block_ref.shape[0]
    rows, dpiece = x_ref.shape
    kpiece = g_ref.shape[1]
    brows = rows // nblk
    own = a_ref.shape[0]
    inner = 2 if ndp % 2 == 0 else 1
    outer = ndp // inner
    nx = nten // 2
    tiles, _, tile = acc.shape
    me, t = lax.axis_index("dp"), lax.axis_index("tensor")
    z, y = lax.div(me, inner), lax.rem(me, inner)
    xx, c = lax.div(t, 2), lax.rem(t, 2)

    def ten_of(rel):
        core = c if rel % 2 == 0 else 1 - c
        return 2 * lax.rem(xx + rel // 2, nx) + core

    def place_there(rel):
        return 2 * ((nx - rel // 2) % nx) + rel % 2

    barrier = pltpu.get_barrier_semaphore()

    def greet_dp(j):
        pl.semaphore_signal(
            barrier, inc=1, device_id=(lax.rem(me + j, ndp), t), device_id_type=MESH
        )

    def greet_ten(j):
        pl.semaphore_signal(
            barrier, inc=1, device_id=(me, lax.rem(t + j, nten)), device_id_type=MESH
        )

    loop(1, ndp, greet_dp)
    loop(1, nten, greet_ten)

    mine = pl.ds(me * own, own)
    local = [
        pltpu.make_async_copy(src, dst, local_sem.at[i])
        for i, (src, dst) in enumerate((
            (tok_ref, tok), (g_ref, gall.at[0]), (owner_ref, owner), (block_ref, block),
            (u_ref, uall.at[mine]), (a_ref, aall.at[mine]), (x_ref, xv),
        ))
    ]
    weights = [
        pltpu.make_async_copy(
            w_ref.at[:, pl.ds(pl.multiple_of(ten_of(rel) * kpiece, kpiece), kpiece)],
            wv.at[:, pl.ds(rel * kpiece, kpiece)], w_sem.at[rel],
        )
        for rel in range(nten)
    ]
    for cp in local[:2] + weights[:1] + local[2:] + weights[1:]:
        cp.start()
    pl.semaphore_wait(barrier, ndp + nten - 2)

    def hop(src, k, way, first):
        slot = src * own + k
        if way == 2:
            to = inner * z + 1 - y
        else:
            to = inner * (z + 1 - 2 * way) + y
        return pltpu.make_async_remote_copy(
            src_ref=(a_ref.at[k] if first else aall.at[slot]),
            dst_ref=aall.at[slot],
            send_sem=a_send.at[way, slot],
            recv_sem=a_recv.at[slot],
            device_id=(to, t),
            device_id_type=MESH,
        )

    def to_peer(j):
        return pltpu.make_async_remote_copy(
            src_ref=u_ref,
            dst_ref=uall.at[mine],
            send_sem=u_send.at[j],
            recv_sem=u_recv.at[j],
            device_id=(lax.rem(me + j, ndp), t),
            device_id_type=MESH,
        )

    def from_peer(j):
        at = pl.ds(lax.rem(me + ndp - j, ndp) * own, own)
        pltpu.make_async_remote_copy(
            src_ref=u_ref,
            dst_ref=uall.at[at],
            send_sem=u_send.at[j],
            recv_sem=u_recv.at[j],
            device_id=(lax.rem(me + j, ndp), t),
            device_id_type=MESH,
        ).wait_recv()

    def for_ways(fn, ways):
        for way in ways:
            if way == 2:
                if inner == 2:
                    fn(2)
            else:
                ok = z + 1 < outer if way == 0 else z > 0
                pl.when(ok)(functools.partial(fn, way))

    def start_hops(src, k, ways, first=False):
        for_ways(lambda way: hop(src, k, way, first).start(), ways)

    def wait_hops(src, k, ways, first=False):
        for_ways(lambda way: hop(src, k, way, first).wait_send(), ways)

    def got_hop(src, k):
        hop(src, k, 0, False).wait_recv()

    def line(d, k, fn):
        pl.when(z - d >= 0)(lambda: fn(inner * (z - d) + y, k, (0, 2)))
        pl.when(z + d < outer)(lambda: fn(inner * (z + d) + y, k, (1, 2)))

    def lines(d, fn):
        for k in range(own):
            line(d, k, fn)

    def span_of(i):
        return pl.ds(i * brows, brows)

    def g_own(rel, i):
        there = place_there(rel)
        return pltpu.make_async_remote_copy(
            src_ref=g_ref.at[span_of(i)],
            dst_ref=gall.at[there, span_of(i)],
            send_sem=g_send.at[rel, i],
            recv_sem=g_recv.at[there, i],
            device_id=(me, ten_of(rel)),
            device_id_type=MESH,
        )

    def g_pass(j, i):
        return pltpu.make_async_remote_copy(
            src_ref=gall.at[2 * j, span_of(i)],
            dst_ref=gall.at[2 * j + 1, span_of(i)],
            send_sem=g_fwd.at[j, i],
            recv_sem=g_recv.at[2 * j + 1, i],
            device_id=(me, ten_of(1)),
            device_id_type=MESH,
        )

    def g_wait(place, i):
        pltpu.make_async_remote_copy(
            src_ref=gall.at[place, span_of(i)],
            dst_ref=gall.at[place, span_of(i)],
            send_sem=g_send.at[0, i],
            recv_sem=g_recv.at[place, i],
            device_id=(me, ten_of(1)),
            device_id_type=MESH,
        ).wait_recv()

    for k in range(own):
        start_hops(me, k, (0, 1, 2), True)
    for i in range(nblk):
        for j in range(1, nx):
            g_own(2 * j, i).start()
    for i in range(nblk):
        g_own(1, i).start()

    local[0].wait()
    live = (tok[...] >= 0).astype(jnp.float32)
    tall = []
    for b in range(nblk):
        lane = live[:, b * brows:(b + 1) * brows]
        col = jnp.broadcast_to(lane, (brows, brows)).T.astype(jnp.bfloat16)
        reps = -(-kpiece // brows)
        tall.append(jnp.concatenate([col] * reps, axis=1)[:, :kpiece])

    def mask_piece(rel):
        for b in range(nblk):
            gm[span_of(b), rel * kpiece:(rel + 1) * kpiece] = gall[rel, span_of(b), :] * tall[b]

    near = 2 * kpiece

    def product(cols, lo, hi):
        return lax.dot_general(
            gm[:, lo:hi], wv[cols, lo:hi], LAST, preferred_element_type=jnp.float32
        )

    def near_product():
        for i in range(nblk):
            g_wait(1, i)
        mask_piece(1)
        for cp in weights[:2]:
            cp.wait()

        def one(n, carry):
            cols = pl.ds(pl.multiple_of(n * tile, tile), tile)
            acc[n] = product(cols, 0, near)
            return carry

        lax.fori_loop(0, tiles, one, 0)

    local[1].wait()
    mask_piece(0)

    def pass_on(src, k, ways):
        got_hop(src, k)
        start_hops(src, k, ways)

    def pass_g(i):
        for j in range(1, nx):
            g_wait(2 * j, i)
            g_pass(j, i).start()

    if outer <= 4:
        for d in range(1, outer):
            lines(d, pass_on)
            if d == 1:
                near_product()
    else:
        near_product()
        loop(1, outer, lambda d: lines(d, pass_on))
    loop(1, ndp, lambda j: to_peer(j).start())

    for cp in local[2:]:
        cp.wait()
    slots = [owner[block[b]] for b in range(nblk)]
    if inner == 2:
        for k in range(own):
            loop(0, outer, lambda d: got_hop(inner * d + 1 - y, k))

    def to_ten(which, rel):
        return pltpu.make_async_remote_copy(
            src_ref=part.at[which, 0], dst_ref=part.at[which, place_there(rel)],
            send_sem=p_send.at[which, rel], recv_sem=p_recv.at[which, place_there(rel)],
            device_id=(me, ten_of(rel)), device_id_type=MESH,
        )

    def from_ten(which, rel):
        pltpu.make_async_remote_copy(
            src_ref=part.at[which, 0], dst_ref=part.at[which, rel],
            send_sem=p_send.at[which, rel], recv_sem=p_recv.at[which, rel],
            device_id=(me, ten_of(rel)), device_id_type=MESH,
        ).wait_recv()

    for which, (pieces, act) in enumerate(((aall, xv), (uall, gall.at[0]))):
        if which == 1:
            loop(1, ndp, from_peer)
        for b in range(nblk):
            span = slice(b * brows, (b + 1) * brows)
            part[which, 0, :, span] = lax.dot_general(
                pieces[slots[b]], act[span, :], LAST, preferred_element_type=jnp.float32
            )
        for rel in range(nten - 1, 0, -1):
            to_ten(which, rel).start()

    for i in range(nblk):
        pass_g(i)
    for j in range(1, nx):
        mask_piece(2 * j)

    def summed(which):
        total = part[which, 0]
        for rel in range(1, nten):
            from_ten(which, rel)
            total = total + part[which, rel]
        return total * live

    lowrank = summed(0).astype(jnp.bfloat16)

    terms = []
    for b in range(nblk):
        span = slice(b * brows, (b + 1) * brows)
        terms.append(
            adapter_scale_factor
            * jnp.dot(lowrank[:, span], gm[span, :kpiece], preferred_element_type=jnp.float32)
        )

    def share(dev, s):
        got = jnp.zeros_like(terms[0])
        for b in range(nblk):
            got = got + jnp.where(slots[b] == dev * own + s, terms[b], 0.0)
        return got

    def to_owner(j):
        return pltpu.make_async_remote_copy(
            src_ref=gsend.at[j], dst_ref=grecv.at[j],
            send_sem=r_send.at[j], recv_sem=r_recv.at[j],
            device_id=(lax.rem(me + j, ndp), t), device_id_type=MESH,
        )

    def scatter(j):
        for s in range(own):
            gsend[j, s] = share(lax.rem(me + j, ndp), s).astype(jnp.bfloat16)
        to_owner(j).start()

    loop(1, ndp, scatter)
    for s in range(own):
        grad_ref[s] = share(me, s)

    for j in range(1, nx):
        for i in range(nblk):
            g_wait(2 * j + 1, i)
        mask_piece(2 * j + 1)
    for cp in weights[2:]:
        cp.wait()
    hidden = summed(1)
    scaled = [
        hidden[:, b * brows:(b + 1) * brows].T.astype(jnp.bfloat16)
        * jnp.bfloat16(adapter_scale_factor)
        for b in range(nblk)
    ]
    kout = wv.shape[1]

    def to_out(n):
        cols = pl.ds(pl.multiple_of(n * tile, tile), tile)
        return pltpu.make_async_copy(outv.at[n], out_ref.at[:, cols], out_sem.at[n])

    def last(n, carry):
        cols = pl.ds(pl.multiple_of(n * tile, tile), tile)
        base = acc[n] + product(cols, near, kout) if nx > 1 else acc[n]
        for b in range(nblk):
            span = slice(b * brows, (b + 1) * brows)
            low = jnp.dot(scaled[b], aall[slots[b], :, cols], preferred_element_type=jnp.float32)
            outv[n, span, :] = (base[span] + low).astype(jnp.bfloat16)
        to_out(n).start()
        return carry

    lax.fori_loop(0, tiles, last, 0)

    for k in range(own):
        wait_hops(me, k, (0, 1, 2), True)
    loop(1, outer, lambda d: lines(d, wait_hops))
    loop(1, ndp, lambda j: to_peer(j).wait_send())
    for i in range(nblk):
        for j in range(1, nx):
            g_own(2 * j, i).wait_send()
            g_pass(j, i).wait_send()
        g_own(1, i).wait_send()
    for which in range(2):
        for rel in range(1, nten):
            to_ten(which, rel).wait_send()

    def gather_grad(j):
        to_owner(j).wait_recv()
        grad_ref[...] += grecv[j].astype(jnp.float32)

    loop(1, ndp, gather_grad)
    loop(1, ndp, lambda j: to_owner(j).wait_send())
    for n in range(tiles):
        to_out(n).wait()


def hand_over(out_ref, grad_ref, out_to, grad_to, out_held, grad_held, sem_in, sem_out):
    parts = sem_in.shape[0] - 1
    rows = out_ref.shape[0] // parts
    ways = [(grad_ref, grad_held, grad_to)]
    for i in range(parts):
        at = pl.ds(i * rows, rows)
        ways.append((out_ref.at[at], out_held.at[at], out_to.at[at]))
    ins = [pltpu.make_async_copy(a, b, sem_in.at[i]) for i, (a, b, _) in enumerate(ways)]
    outs = [pltpu.make_async_copy(b, c, sem_out.at[i]) for i, (_, b, c) in enumerate(ways)]
    for cp in ins:
        cp.start()
    for cp, then in zip(ins, outs):
        cp.wait()
        then.start()
    for cp in outs:
        cp.wait()


def on_device(
    ndp, nten, inputs, cotangent, base_weight, down_a, up_b, block_adapter, token_adapter, owner_map
):
    rows, dpiece = inputs.shape
    kpiece = cotangent.shape[1]
    nblk = block_adapter.shape[0]
    own, rank = up_b.shape[:2]
    slots = own * ndp
    kout = base_weight.shape[1]
    nx = nten // 2
    tile = 256 if dpiece % 256 == 0 else 128
    bf16, f32 = jnp.bfloat16, jnp.float32
    hbm = pl.BlockSpec(memory_space=pltpu.HBM)
    dma = pltpu.SemaphoreType.DMA
    results = pl.pallas_call(
        functools.partial(kernel, ndp, nten),
        out_shape=(
            jax.ShapeDtypeStruct((rows, dpiece), bf16),
            jax.ShapeDtypeStruct((own, rank, kpiece), f32),
        ),
        in_specs=[hbm] * 8,
        out_specs=(pl.BlockSpec(memory_space=pl.ANY), pl.BlockSpec(memory_space=pltpu.VMEM)),
        scratch_shapes=[
            pltpu.SMEM(owner_map.shape, jnp.int32),
            pltpu.SMEM((nblk,), jnp.int32),
            pltpu.VMEM((1, rows), jnp.int32),
            pltpu.VMEM((rows, dpiece), bf16),
            pltpu.VMEM((dpiece, kout), bf16),
            pltpu.VMEM((nten, rows, kpiece), bf16),
            pltpu.VMEM((rows, kout), bf16),
            pltpu.VMEM((dpiece // tile, rows, tile), f32),
            pltpu.VMEM((slots, rank, dpiece), bf16),
            pltpu.VMEM((slots, rank, kpiece), bf16),
            pltpu.VMEM((2, nten, rank, rows), f32),
            pltpu.VMEM((dpiece // tile, rows, tile), bf16),
            pltpu.VMEM((ndp, own, rank, kpiece), bf16),
            pltpu.VMEM((ndp, own, rank, kpiece), bf16),
            dma((7,)),
            dma((nten,)),
            dma((dpiece // tile,)),
            dma((3, slots)),
            dma((slots,)),
            dma((ndp,)),
            dma((ndp,)),
            dma((nten, nblk)),
            dma((nx, nblk)),
            dma((nten, nblk)),
            dma((2, nten)),
            dma((2, nten)),
            dma((ndp,)),
            dma((ndp,)),
        ],
        cost_estimate=pl.CostEstimate(
            flops=2 * rows * dpiece * (kout + 2 * rank),
            bytes_accessed=2 * (2 * rows * dpiece + dpiece * kout + rows * kpiece),
            transcendentals=0,
        ),
        compiler_params=pltpu.CompilerParams(
            collective_id=0, has_side_effects=True, vmem_limit_bytes=64 * 2**20 - 2**18
        ),
    )(
        owner_map, block_adapter, token_adapter.reshape(1, rows), inputs, cotangent, base_weight,
        jnp.swapaxes(down_a, 1, 2), up_b,
    )
    return pl.pallas_call(
        hand_over,
        out_shape=tuple(jax.ShapeDtypeStruct(r.shape, r.dtype) for r in results),
        in_specs=[hbm] * 2,
        out_specs=(hbm, hbm),
        scratch_shapes=[
            pltpu.VMEM((rows, dpiece), bf16),
            pltpu.VMEM((own, rank, kpiece), f32),
            dma((nblk + 1,)),
            dma((nblk + 1,)),
        ],
        cost_estimate=pl.CostEstimate(
            flops=0, bytes_accessed=4 * rows * dpiece, transcendentals=0
        ),
        compiler_params=pltpu.CompilerParams(vmem_limit_bytes=64 * 2**20 - 2**18),
    )(*results)


def solution(mesh):
    in_specs = (
        P("dp", "tensor"),
        P("dp", "tensor"),
        P("tensor", None),
        P("dp", "tensor", None),
        P("dp", None, "tensor"),
        P("dp"),
        P("dp"),
        P(),
    )
    out_specs = (P("dp", "tensor"), P("dp", None, "tensor"))
    return jax.shard_map(
        functools.partial(on_device, mesh.shape["dp"], mesh.shape["tensor"]),
        mesh=mesh, in_specs=in_specs, out_specs=out_specs, check_vma=False,
    )
```

```python
import functools

import jax
import jax.numpy as jnp
from jax import lax
from jax.experimental import pallas as pl
from jax.experimental.pallas import tpu as pltpu
from jax.sharding import PartitionSpec as P

adapter_scale_factor = 2.0
MESH = pl.DeviceIdType.MESH
LAST = (((1,), (1,)), ((), ()))
FIRST = (((0,), (0,)), ((), ()))


def loop(lo, hi, body):
    if hi - lo <= 8:
        for i in range(lo, hi):
            body(i)
    else:
        lax.fori_loop(lo, hi, lambda i, c: (body(i), c)[1], 0)


def kernel(
    ndp, nten, owner_ref, block_ref, tok_ref, x_ref, g_ref, w_ref, a_ref, u_ref,
    out_ref, grad_ref,
    owner, block, tok, xv, wv, gall, gm, acc, aall, uall, part, outv, gsend, grecv,
    local_sem, w_sem, out_sem, a_send, a_recv, u_send, u_recv, g_send, g_fwd, g_recv,
    p_send, p_recv, r_send, r_recv,
):
    nblk = block_ref.shape[0]
    rows, dpiece = x_ref.shape
    kpiece = g_ref.shape[1]
    brows = rows // nblk
    own = a_ref.shape[0]
    inner = 2 if ndp % 2 == 0 else 1
    outer = ndp // inner
    nx = nten // 2
    tiles, _, tile = acc.shape
    me, t = lax.axis_index("dp"), lax.axis_index("tensor")
    z, y = lax.div(me, inner), lax.rem(me, inner)
    xx, c = lax.div(t, 2), lax.rem(t, 2)

    def ten_of(rel):
        core = c if rel % 2 == 0 else 1 - c
        return 2 * lax.rem(xx + rel // 2, nx) + core

    def place_there(rel):
        return 2 * ((nx - rel // 2) % nx) + rel % 2

    barrier = pltpu.get_barrier_semaphore()

    def greet_dp(j):
        pl.semaphore_signal(
            barrier, inc=1, device_id=(lax.rem(me + j, ndp), t), device_id_type=MESH
        )

    def greet_ten(j):
        pl.semaphore_signal(
            barrier, inc=1, device_id=(me, lax.rem(t + j, nten)), device_id_type=MESH
        )

    loop(1, ndp, greet_dp)
    loop(1, nten, greet_ten)

    mine = pl.ds(me * own, own)
    local = [
        pltpu.make_async_copy(src, dst, local_sem.at[i])
        for i, (src, dst) in enumerate((
            (tok_ref, tok), (g_ref, gall.at[0]), (owner_ref, owner), (block_ref, block),
            (u_ref, uall.at[mine]), (a_ref, aall.at[mine]), (x_ref, xv),
        ))
    ]
    weights = [
        pltpu.make_async_copy(
            w_ref.at[:, pl.ds(pl.multiple_of(ten_of(rel) * kpiece, kpiece), kpiece)],
            wv.at[:, pl.ds(rel * kpiece, kpiece)], w_sem.at[rel],
        )
        for rel in range(nten)
    ]
    for cp in local[:2] + weights[:1] + local[2:] + weights[1:]:
        cp.start()
    pl.semaphore_wait(barrier, ndp + nten - 2)

    def hop(src, k, way, first):
        slot = src * own + k
        if way == 2:
            to = inner * z + 1 - y
        else:
            to = inner * (z + 1 - 2 * way) + y
        return pltpu.make_async_remote_copy(
            src_ref=(a_ref.at[k] if first else aall.at[slot]),
            dst_ref=aall.at[slot],
            send_sem=a_send.at[way, slot],
            recv_sem=a_recv.at[slot],
            device_id=(to, t),
            device_id_type=MESH,
        )

    def to_peer(j):
        return pltpu.make_async_remote_copy(
            src_ref=u_ref,
            dst_ref=uall.at[mine],
            send_sem=u_send.at[j],
            recv_sem=u_recv.at[j],
            device_id=(lax.rem(me + j, ndp), t),
            device_id_type=MESH,
        )

    def from_peer(j):
        at = pl.ds(lax.rem(me + ndp - j, ndp) * own, own)
        pltpu.make_async_remote_copy(
            src_ref=u_ref,
            dst_ref=uall.at[at],
            send_sem=u_send.at[j],
            recv_sem=u_recv.at[j],
            device_id=(lax.rem(me + j, ndp), t),
            device_id_type=MESH,
        ).wait_recv()

    def for_ways(fn, ways):
        for way in ways:
            if way == 2:
                if inner == 2:
                    fn(2)
            else:
                ok = z + 1 < outer if way == 0 else z > 0
                pl.when(ok)(functools.partial(fn, way))

    def start_hops(src, k, ways, first=False):
        for_ways(lambda way: hop(src, k, way, first).start(), ways)

    def wait_hops(src, k, ways, first=False):
        for_ways(lambda way: hop(src, k, way, first).wait_send(), ways)

    def got_hop(src, k):
        hop(src, k, 0, False).wait_recv()

    def line(d, k, fn):
        pl.when(z - d >= 0)(lambda: fn(inner * (z - d) + y, k, (0, 2)))
        pl.when(z + d < outer)(lambda: fn(inner * (z + d) + y, k, (1, 2)))

    def lines(d, fn):
        for k in range(own):
            line(d, k, fn)

    def span_of(i):
        return pl.ds(i * brows, brows)

    def g_own(rel, i):
        there = place_there(rel)
        return pltpu.make_async_remote_copy(
            src_ref=g_ref.at[span_of(i)],
            dst_ref=gall.at[there, span_of(i)],
            send_sem=g_send.at[rel, i],
            recv_sem=g_recv.at[there, i],
            device_id=(me, ten_of(rel)),
            device_id_type=MESH,
        )

    def g_pass(j, i):
        return pltpu.make_async_remote_copy(
            src_ref=gall.at[2 * j, span_of(i)],
            dst_ref=gall.at[2 * j + 1, span_of(i)],
            send_sem=g_fwd.at[j, i],
            recv_sem=g_recv.at[2 * j + 1, i],
            device_id=(me, ten_of(1)),
            device_id_type=MESH,
        )

    def g_wait(place, i):
        pltpu.make_async_remote_copy(
            src_ref=gall.at[place, span_of(i)],
            dst_ref=gall.at[place, span_of(i)],
            send_sem=g_send.at[0, i],
            recv_sem=g_recv.at[place, i],
            device_id=(me, ten_of(1)),
            device_id_type=MESH,
        ).wait_recv()

    for k in range(own):
        start_hops(me, k, (0, 1, 2), True)
    for i in range(nblk):
        for j in range(1, nx):
            g_own(2 * j, i).start()
    for i in range(nblk):
        g_own(1, i).start()

    local[0].wait()
    live = (tok[...] >= 0).astype(jnp.float32)
    tall = []
    for b in range(nblk):
        lane = live[:, b * brows:(b + 1) * brows]
        col = jnp.broadcast_to(lane, (brows, brows)).T.astype(jnp.bfloat16)
        reps = -(-kpiece // brows)
        tall.append(jnp.concatenate([col] * reps, axis=1)[:, :kpiece])

    def mask_piece(rel):
        for b in range(nblk):
            gm[span_of(b), rel * kpiece:(rel + 1) * kpiece] = gall[rel, span_of(b), :] * tall[b]

    near = 2 * kpiece

    def product(cols, lo, hi):
        return lax.dot_general(
            gm[:, lo:hi], wv[cols, lo:hi], LAST, preferred_element_type=jnp.float32
        )

    def near_product():
        for i in range(nblk):
            g_wait(1, i)
        mask_piece(1)
        for cp in weights[:2]:
            cp.wait()

        def one(n, carry):
            cols = pl.ds(pl.multiple_of(n * tile, tile), tile)
            acc[n] = product(cols, 0, near)
            return carry

        lax.fori_loop(0, tiles, one, 0)

    local[1].wait()
    mask_piece(0)

    def pass_on(src, k, ways):
        got_hop(src, k)
        start_hops(src, k, ways)

    def pass_g(i):
        for j in range(1, nx):
            g_wait(2 * j, i)
            g_pass(j, i).start()

    if outer <= 4:
        for d in range(1, outer):
            lines(d, pass_on)
            if d == 1:
                near_product()
    else:
        near_product()
        loop(1, outer, lambda d: lines(d, pass_on))
    for cp in local[2:]:
        cp.wait()
    slots = [owner[block[b]] for b in range(nblk)]
    if inner == 2:
        for k in range(own):
            loop(0, outer, lambda d: got_hop(inner * d + 1 - y, k))

    def to_ten(which, rel):
        return pltpu.make_async_remote_copy(
            src_ref=part.at[which, 0], dst_ref=part.at[which, place_there(rel)],
            send_sem=p_send.at[which, rel], recv_sem=p_recv.at[which, place_there(rel)],
            device_id=(me, ten_of(rel)), device_id_type=MESH,
        )

    def from_ten(which, rel):
        pltpu.make_async_remote_copy(
            src_ref=part.at[which, 0], dst_ref=part.at[which, rel],
            send_sem=p_send.at[which, rel], recv_sem=p_recv.at[which, rel],
            device_id=(me, ten_of(rel)), device_id_type=MESH,
        ).wait_recv()

    def send_partial(which, pieces, act):
        for b in range(nblk):
            span = slice(b * brows, (b + 1) * brows)
            part[which, 0, :, span] = lax.dot_general(
                pieces[slots[b]], act[span, :], LAST, preferred_element_type=jnp.float32
            )
        for rel in range(nten - 1, 0, -1):
            to_ten(which, rel).start()

    send_partial(0, aall, xv)
    loop(1, ndp, lambda j: to_peer(j).start())

    for i in range(nblk):
        pass_g(i)
    for j in range(1, nx):
        mask_piece(2 * j)

    def summed(which):
        total = part[which, 0]
        for rel in range(1, nten):
            from_ten(which, rel)
            total = total + part[which, rel]
        return total * live

    lowrank = summed(0).astype(jnp.bfloat16)

    terms = []
    for b in range(nblk):
        span = slice(b * brows, (b + 1) * brows)
        terms.append(
            adapter_scale_factor
            * jnp.dot(lowrank[:, span], gm[span, :kpiece], preferred_element_type=jnp.float32)
        )

    def share(dev, s):
        got = jnp.zeros_like(terms[0])
        for b in range(nblk):
            got = got + jnp.where(slots[b] == dev * own + s, terms[b], 0.0)
        return got

    def to_owner(j):
        return pltpu.make_async_remote_copy(
            src_ref=gsend.at[j], dst_ref=grecv.at[j],
            send_sem=r_send.at[j], recv_sem=r_recv.at[j],
            device_id=(lax.rem(me + j, ndp), t), device_id_type=MESH,
        )

    def scatter(j):
        for s in range(own):
            gsend[j, s] = share(lax.rem(me + j, ndp), s).astype(jnp.bfloat16)
        to_owner(j).start()

    loop(1, ndp, scatter)
    for s in range(own):
        grad_ref[s] = share(me, s)

    loop(1, ndp, from_peer)
    send_partial(1, uall, gall.at[0])
    for j in range(1, nx):
        for i in range(nblk):
            g_wait(2 * j + 1, i)
        mask_piece(2 * j + 1)
    for cp in weights[2:]:
        cp.wait()
    kout = wv.shape[1]

    def far_product(n, carry):
        cols = pl.ds(pl.multiple_of(n * tile, tile), tile)
        acc[n] += product(cols, near, kout)
        return carry

    if nx > 1:
        lax.fori_loop(0, tiles, far_product, 0)
    hidden = summed(1)
    scaled = [
        hidden[:, b * brows:(b + 1) * brows].T.astype(jnp.bfloat16)
        * jnp.bfloat16(adapter_scale_factor)
        for b in range(nblk)
    ]

    def to_out(n):
        cols = pl.ds(pl.multiple_of(n * tile, tile), tile)
        return pltpu.make_async_copy(outv.at[n], out_ref.at[:, cols], out_sem.at[n])

    def last(n, carry):
        cols = pl.ds(pl.multiple_of(n * tile, tile), tile)
        for b in range(nblk):
            span = slice(b * brows, (b + 1) * brows)
            low = jnp.dot(scaled[b], aall[slots[b], :, cols], preferred_element_type=jnp.float32)
            outv[n, span, :] = (acc[n, span, :] + low).astype(jnp.bfloat16)
        to_out(n).start()
        return carry

    lax.fori_loop(0, tiles, last, 0)

    for k in range(own):
        wait_hops(me, k, (0, 1, 2), True)
    loop(1, outer, lambda d: lines(d, wait_hops))
    loop(1, ndp, lambda j: to_peer(j).wait_send())
    for i in range(nblk):
        for j in range(1, nx):
            g_own(2 * j, i).wait_send()
            g_pass(j, i).wait_send()
        g_own(1, i).wait_send()
    for which in range(2):
        for rel in range(1, nten):
            to_ten(which, rel).wait_send()

    def gather_grad(j):
        to_owner(j).wait_recv()
        grad_ref[...] += grecv[j].astype(jnp.float32)

    loop(1, ndp, gather_grad)
    loop(1, ndp, lambda j: to_owner(j).wait_send())
    for n in range(tiles):
        to_out(n).wait()


def hand_over(out_ref, grad_ref, out_to, grad_to, out_held, grad_held, sem_in, sem_out):
    parts = sem_in.shape[0] - 1
    rows = out_ref.shape[0] // parts
    ways = [(grad_ref, grad_held, grad_to)]
    for i in range(parts):
        at = pl.ds(i * rows, rows)
        ways.append((out_ref.at[at], out_held.at[at], out_to.at[at]))
    ins = [pltpu.make_async_copy(a, b, sem_in.at[i]) for i, (a, b, _) in enumerate(ways)]
    outs = [pltpu.make_async_copy(b, c, sem_out.at[i]) for i, (_, b, c) in enumerate(ways)]
    for cp in ins:
        cp.start()
    for cp, then in zip(ins, outs):
        cp.wait()
        then.start()
    for cp in outs:
        cp.wait()


def on_device(
    ndp, nten, inputs, cotangent, base_weight, down_a, up_b, block_adapter, token_adapter, owner_map
):
    rows, dpiece = inputs.shape
    kpiece = cotangent.shape[1]
    nblk = block_adapter.shape[0]
    own, rank = up_b.shape[:2]
    slots = own * ndp
    kout = base_weight.shape[1]
    nx = nten // 2
    tile = 256 if dpiece % 256 == 0 else 128
    bf16, f32 = jnp.bfloat16, jnp.float32
    hbm = pl.BlockSpec(memory_space=pltpu.HBM)
    dma = pltpu.SemaphoreType.DMA
    results = pl.pallas_call(
        functools.partial(kernel, ndp, nten),
        out_shape=(
            jax.ShapeDtypeStruct((rows, dpiece), bf16),
            jax.ShapeDtypeStruct((own, rank, kpiece), f32),
        ),
        in_specs=[hbm] * 8,
        out_specs=(pl.BlockSpec(memory_space=pl.ANY), pl.BlockSpec(memory_space=pltpu.VMEM)),
        scratch_shapes=[
            pltpu.SMEM(owner_map.shape, jnp.int32),
            pltpu.SMEM((nblk,), jnp.int32),
            pltpu.VMEM((1, rows), jnp.int32),
            pltpu.VMEM((rows, dpiece), bf16),
            pltpu.VMEM((dpiece, kout), bf16),
            pltpu.VMEM((nten, rows, kpiece), bf16),
            pltpu.VMEM((rows, kout), bf16),
            pltpu.VMEM((dpiece // tile, rows, tile), f32),
            pltpu.VMEM((slots, rank, dpiece), bf16),
            pltpu.VMEM((slots, rank, kpiece), bf16),
            pltpu.VMEM((2, nten, rank, rows), f32),
            pltpu.VMEM((dpiece // tile, rows, tile), bf16),
            pltpu.VMEM((ndp, own, rank, kpiece), bf16),
            pltpu.VMEM((ndp, own, rank, kpiece), bf16),
            dma((7,)),
            dma((nten,)),
            dma((dpiece // tile,)),
            dma((3, slots)),
            dma((slots,)),
            dma((ndp,)),
            dma((ndp,)),
            dma((nten, nblk)),
            dma((nx, nblk)),
            dma((nten, nblk)),
            dma((2, nten)),
            dma((2, nten)),
            dma((ndp,)),
            dma((ndp,)),
        ],
        cost_estimate=pl.CostEstimate(
            flops=2 * rows * dpiece * (kout + 2 * rank),
            bytes_accessed=2 * (2 * rows * dpiece + dpiece * kout + rows * kpiece),
            transcendentals=0,
        ),
        compiler_params=pltpu.CompilerParams(
            collective_id=0, has_side_effects=True, vmem_limit_bytes=64 * 2**20 - 2**18
        ),
    )(
        owner_map, block_adapter, token_adapter.reshape(1, rows), inputs, cotangent, base_weight,
        jnp.swapaxes(down_a, 1, 2), up_b,
    )
    return pl.pallas_call(
        hand_over,
        out_shape=tuple(jax.ShapeDtypeStruct(r.shape, r.dtype) for r in results),
        in_specs=[hbm] * 2,
        out_specs=(hbm, hbm),
        scratch_shapes=[
            pltpu.VMEM((rows, dpiece), bf16),
            pltpu.VMEM((own, rank, kpiece), f32),
            dma((nblk + 1,)),
            dma((nblk + 1,)),
        ],
        cost_estimate=pl.CostEstimate(
            flops=0, bytes_accessed=4 * rows * dpiece, transcendentals=0
        ),
        compiler_params=pltpu.CompilerParams(vmem_limit_bytes=64 * 2**20 - 2**18),
    )(*results)


def solution(mesh):
    in_specs = (
        P("dp", "tensor"),
        P("dp", "tensor"),
        P("tensor", None),
        P("dp", "tensor", None),
        P("dp", None, "tensor"),
        P("dp"),
        P("dp"),
        P(),
    )
    out_specs = (P("dp", "tensor"), P("dp", None, "tensor"))
    return jax.shard_map(
        functools.partial(on_device, mesh.shape["dp"], mesh.shape["tensor"]),
        mesh=mesh, in_specs=in_specs, out_specs=out_specs, check_vma=False,
    )
```

```python
import functools

import jax
import jax.numpy as jnp
from jax import lax
from jax.experimental import pallas as pl
from jax.experimental.pallas import tpu as pltpu
from jax.sharding import PartitionSpec as P

adapter_scale_factor = 2.0
MESH = pl.DeviceIdType.MESH
LAST = (((1,), (1,)), ((), ()))
FIRST = (((0,), (0,)), ((), ()))


def loop(lo, hi, body):
    if hi - lo <= 8:
        for i in range(lo, hi):
            body(i)
    else:
        lax.fori_loop(lo, hi, lambda i, c: (body(i), c)[1], 0)


def kernel(
    ndp, nten, owner_ref, block_ref, tok_ref, x_ref, g_ref, w_ref, a_ref, u_ref,
    out_ref, grad_ref,
    owner, block, tok, xv, wv, gall, gm, acc, aall, uall, part, outv, gsend, grecv,
    local_sem, w_sem, out_sem, a_send, a_recv, u_send, u_recv, g_send, g_fwd, g_recv,
    p_send, p_recv, r_send, r_recv,
):
    nblk = block_ref.shape[0]
    rows, dpiece = x_ref.shape
    kpiece = g_ref.shape[1]
    brows = rows // nblk
    own = a_ref.shape[0]
    inner = 2 if ndp % 2 == 0 else 1
    outer = ndp // inner
    nx = nten // 2
    tiles, _, tile = acc.shape
    me, t = lax.axis_index("dp"), lax.axis_index("tensor")
    z, y = lax.div(me, inner), lax.rem(me, inner)
    xx, c = lax.div(t, 2), lax.rem(t, 2)

    def ten_of(rel):
        core = c if rel % 2 == 0 else 1 - c
        return 2 * lax.rem(xx + rel // 2, nx) + core

    def place_there(rel):
        return 2 * ((nx - rel // 2) % nx) + rel % 2

    barrier = pltpu.get_barrier_semaphore()

    def greet_dp(j):
        pl.semaphore_signal(
            barrier, inc=1, device_id=(lax.rem(me + j, ndp), t), device_id_type=MESH
        )

    def greet_ten(j):
        pl.semaphore_signal(
            barrier, inc=1, device_id=(me, lax.rem(t + j, nten)), device_id_type=MESH
        )

    loop(1, ndp, greet_dp)
    loop(1, nten, greet_ten)

    mine = pl.ds(me * own, own)
    local = [
        pltpu.make_async_copy(src, dst, local_sem.at[i])
        for i, (src, dst) in enumerate((
            (tok_ref, tok), (g_ref, gall.at[0]), (owner_ref, owner), (block_ref, block),
            (u_ref, uall.at[mine]), (a_ref, aall.at[mine]), (x_ref, xv),
        ))
    ]
    weights = [
        pltpu.make_async_copy(
            w_ref.at[:, pl.ds(pl.multiple_of(ten_of(rel) * kpiece, kpiece), kpiece)],
            wv.at[:, pl.ds(rel * kpiece, kpiece)], w_sem.at[rel],
        )
        for rel in range(nten)
    ]
    for cp in local[:2] + weights[:1] + local[2:] + weights[1:]:
        cp.start()
    pl.semaphore_wait(barrier, ndp + nten - 2)

    def hop(src, k, way, first):
        slot = src * own + k
        if way == 2:
            to = inner * z + 1 - y
        else:
            to = inner * (z + 1 - 2 * way) + y
        return pltpu.make_async_remote_copy(
            src_ref=(a_ref.at[k] if first else aall.at[slot]),
            dst_ref=aall.at[slot],
            send_sem=a_send.at[way, slot],
            recv_sem=a_recv.at[slot],
            device_id=(to, t),
            device_id_type=MESH,
        )

    def to_peer(j):
        return pltpu.make_async_remote_copy(
            src_ref=u_ref,
            dst_ref=uall.at[mine],
            send_sem=u_send.at[j],
            recv_sem=u_recv.at[j],
            device_id=(lax.rem(me + j, ndp), t),
            device_id_type=MESH,
        )

    def from_peer(j):
        at = pl.ds(lax.rem(me + ndp - j, ndp) * own, own)
        pltpu.make_async_remote_copy(
            src_ref=u_ref,
            dst_ref=uall.at[at],
            send_sem=u_send.at[j],
            recv_sem=u_recv.at[j],
            device_id=(lax.rem(me + j, ndp), t),
            device_id_type=MESH,
        ).wait_recv()

    def for_ways(fn, ways):
        for way in ways:
            if way == 2:
                if inner == 2:
                    fn(2)
            else:
                ok = z + 1 < outer if way == 0 else z > 0
                pl.when(ok)(functools.partial(fn, way))

    def start_hops(src, k, ways, first=False):
        for_ways(lambda way: hop(src, k, way, first).start(), ways)

    def wait_hops(src, k, ways, first=False):
        for_ways(lambda way: hop(src, k, way, first).wait_send(), ways)

    def got_hop(src, k):
        hop(src, k, 0, False).wait_recv()

    def line(d, k, fn):
        pl.when(z - d >= 0)(lambda: fn(inner * (z - d) + y, k, (0, 2)))
        pl.when(z + d < outer)(lambda: fn(inner * (z + d) + y, k, (1, 2)))

    def lines(d, fn):
        for k in range(own):
            line(d, k, fn)

    def span_of(i):
        return pl.ds(i * brows, brows)

    def g_own(rel, i):
        there = place_there(rel)
        return pltpu.make_async_remote_copy(
            src_ref=g_ref.at[span_of(i)],
            dst_ref=gall.at[there, span_of(i)],
            send_sem=g_send.at[rel, i],
            recv_sem=g_recv.at[there, i],
            device_id=(me, ten_of(rel)),
            device_id_type=MESH,
        )

    def g_pass(j, i):
        return pltpu.make_async_remote_copy(
            src_ref=gall.at[2 * j, span_of(i)],
            dst_ref=gall.at[2 * j + 1, span_of(i)],
            send_sem=g_fwd.at[j, i],
            recv_sem=g_recv.at[2 * j + 1, i],
            device_id=(me, ten_of(1)),
            device_id_type=MESH,
        )

    def g_wait(place, i):
        pltpu.make_async_remote_copy(
            src_ref=gall.at[place, span_of(i)],
            dst_ref=gall.at[place, span_of(i)],
            send_sem=g_send.at[0, i],
            recv_sem=g_recv.at[place, i],
            device_id=(me, ten_of(1)),
            device_id_type=MESH,
        ).wait_recv()

    for k in range(own):
        start_hops(me, k, (0, 1), True)
    loop(1, ndp, lambda j: to_peer(j).start())
    for k in range(own):
        start_hops(me, k, (2,), True)
    for i in range(nblk):
        for j in range(1, nx):
            g_own(2 * j, i).start()
    for i in range(nblk):
        g_own(1, i).start()

    local[0].wait()
    live = (tok[...] >= 0).astype(jnp.float32)
    tall = []
    for b in range(nblk):
        lane = live[:, b * brows:(b + 1) * brows]
        col = jnp.broadcast_to(lane, (brows, brows)).T.astype(jnp.bfloat16)
        reps = -(-kpiece // brows)
        tall.append(jnp.concatenate([col] * reps, axis=1)[:, :kpiece])

    def mask_piece(rel):
        for b in range(nblk):
            gm[span_of(b), rel * kpiece:(rel + 1) * kpiece] = gall[rel, span_of(b), :] * tall[b]

    near = 2 * kpiece

    def product(cols, lo, hi):
        return lax.dot_general(
            gm[:, lo:hi], wv[cols, lo:hi], LAST, preferred_element_type=jnp.float32
        )

    def near_product():
        for i in range(nblk):
            g_wait(1, i)
        mask_piece(1)
        for cp in weights[:2]:
            cp.wait()

        def one(n, carry):
            cols = pl.ds(pl.multiple_of(n * tile, tile), tile)
            acc[n] = product(cols, 0, near)
            return carry

        lax.fori_loop(0, tiles, one, 0)

    local[1].wait()
    mask_piece(0)

    def pass_on(src, k, ways):
        got_hop(src, k)
        start_hops(src, k, ways)

    def pass_g(i):
        for j in range(1, nx):
            g_wait(2 * j, i)
            g_pass(j, i).start()

    def to_ten(which, rel):
        return pltpu.make_async_remote_copy(
            src_ref=part.at[which, 0], dst_ref=part.at[which, place_there(rel)],
            send_sem=p_send.at[which, rel], recv_sem=p_recv.at[which, place_there(rel)],
            device_id=(me, ten_of(rel)), device_id_type=MESH,
        )

    def from_ten(which, rel):
        pltpu.make_async_remote_copy(
            src_ref=part.at[which, 0], dst_ref=part.at[which, rel],
            send_sem=p_send.at[which, rel], recv_sem=p_recv.at[which, rel],
            device_id=(me, ten_of(rel)), device_id_type=MESH,
        ).wait_recv()

    def send_partial(which, pieces, act):
        for b in range(nblk):
            span = slice(b * brows, (b + 1) * brows)
            part[which, 0, :, span] = lax.dot_general(
                pieces[slots[b]], act[span, :], LAST, preferred_element_type=jnp.float32
            )
        for rel in range(nten - 1, 0, -1):
            to_ten(which, rel).start()

    for cp in local[2:]:
        cp.wait()
    slots = [owner[block[b]] for b in range(nblk)]
    if outer <= 4:
        if outer < 2:
            near_product()
        for d in range(1, outer):
            lines(d, pass_on)
            if d == 1:
                near_product()
    else:
        near_product()
        loop(1, outer, lambda d: lines(d, pass_on))
    loop(1, ndp, from_peer)
    send_partial(1, uall, gall.at[0])
    if inner == 2:
        for k in range(own):
            loop(0, outer, lambda d: got_hop(inner * d + 1 - y, k))

    send_partial(0, aall, xv)

    for i in range(nblk):
        pass_g(i)
    for j in range(1, nx):
        mask_piece(2 * j)

    def summed(which):
        total = part[which, 0]
        for rel in range(1, nten):
            from_ten(which, rel)
            total = total + part[which, rel]
        return total * live

    lowrank = summed(0).astype(jnp.bfloat16)

    terms = []
    for b in range(nblk):
        span = slice(b * brows, (b + 1) * brows)
        terms.append(
            adapter_scale_factor
            * jnp.dot(lowrank[:, span], gm[span, :kpiece], preferred_element_type=jnp.float32)
        )

    def share(dev, s):
        got = jnp.zeros_like(terms[0])
        for b in range(nblk):
            got = got + jnp.where(slots[b] == dev * own + s, terms[b], 0.0)
        return got

    def to_owner(j):
        return pltpu.make_async_remote_copy(
            src_ref=gsend.at[j], dst_ref=grecv.at[j],
            send_sem=r_send.at[j], recv_sem=r_recv.at[j],
            device_id=(lax.rem(me + j, ndp), t), device_id_type=MESH,
        )

    def scatter(j):
        for s in range(own):
            gsend[j, s] = share(lax.rem(me + j, ndp), s).astype(jnp.bfloat16)
        to_owner(j).start()

    loop(1, ndp, scatter)
    for s in range(own):
        grad_ref[s] = share(me, s)

    for j in range(1, nx):
        for i in range(nblk):
            g_wait(2 * j + 1, i)
        mask_piece(2 * j + 1)
    for cp in weights[2:]:
        cp.wait()
    hidden = summed(1)
    scaled = [
        hidden[:, b * brows:(b + 1) * brows].T.astype(jnp.bfloat16)
        * jnp.bfloat16(adapter_scale_factor)
        for b in range(nblk)
    ]
    kout = wv.shape[1]

    def to_out(n):
        cols = pl.ds(pl.multiple_of(n * tile, tile), tile)
        return pltpu.make_async_copy(outv.at[n], out_ref.at[:, cols], out_sem.at[n])

    def last(n, carry):
        cols = pl.ds(pl.multiple_of(n * tile, tile), tile)
        base = acc[n] + product(cols, near, kout) if nx > 1 else acc[n]
        for b in range(nblk):
            span = slice(b * brows, (b + 1) * brows)
            low = jnp.dot(scaled[b], aall[slots[b], :, cols], preferred_element_type=jnp.float32)
            outv[n, span, :] = (base[span] + low).astype(jnp.bfloat16)
        to_out(n).start()
        return carry

    lax.fori_loop(0, tiles, last, 0)

    for k in range(own):
        wait_hops(me, k, (0, 1, 2), True)
    loop(1, outer, lambda d: lines(d, wait_hops))
    loop(1, ndp, lambda j: to_peer(j).wait_send())
    for i in range(nblk):
        for j in range(1, nx):
            g_own(2 * j, i).wait_send()
            g_pass(j, i).wait_send()
        g_own(1, i).wait_send()
    for which in range(2):
        for rel in range(1, nten):
            to_ten(which, rel).wait_send()

    def gather_grad(j):
        to_owner(j).wait_recv()
        grad_ref[...] += grecv[j].astype(jnp.float32)

    loop(1, ndp, gather_grad)
    loop(1, ndp, lambda j: to_owner(j).wait_send())
    for n in range(tiles):
        to_out(n).wait()


def hand_over(out_ref, grad_ref, out_to, grad_to, out_held, grad_held, sem_in, sem_out):
    parts = sem_in.shape[0] - 1
    rows = out_ref.shape[0] // parts
    ways = [(grad_ref, grad_held, grad_to)]
    for i in range(parts):
        at = pl.ds(i * rows, rows)
        ways.append((out_ref.at[at], out_held.at[at], out_to.at[at]))
    ins = [pltpu.make_async_copy(a, b, sem_in.at[i]) for i, (a, b, _) in enumerate(ways)]
    outs = [pltpu.make_async_copy(b, c, sem_out.at[i]) for i, (_, b, c) in enumerate(ways)]
    for cp in ins:
        cp.start()
    for cp, then in zip(ins, outs):
        cp.wait()
        then.start()
    for cp in outs:
        cp.wait()


def on_device(
    ndp, nten, inputs, cotangent, base_weight, down_a, up_b, block_adapter, token_adapter, owner_map
):
    rows, dpiece = inputs.shape
    kpiece = cotangent.shape[1]
    nblk = block_adapter.shape[0]
    own, rank = up_b.shape[:2]
    slots = own * ndp
    kout = base_weight.shape[1]
    nx = nten // 2
    tile = 256 if dpiece % 256 == 0 else 128
    bf16, f32 = jnp.bfloat16, jnp.float32
    hbm = pl.BlockSpec(memory_space=pltpu.HBM)
    dma = pltpu.SemaphoreType.DMA
    results = pl.pallas_call(
        functools.partial(kernel, ndp, nten),
        out_shape=(
            jax.ShapeDtypeStruct((rows, dpiece), bf16),
            jax.ShapeDtypeStruct((own, rank, kpiece), f32),
        ),
        in_specs=[hbm] * 8,
        out_specs=(pl.BlockSpec(memory_space=pl.ANY), pl.BlockSpec(memory_space=pltpu.VMEM)),
        scratch_shapes=[
            pltpu.SMEM(owner_map.shape, jnp.int32),
            pltpu.SMEM((nblk,), jnp.int32),
            pltpu.VMEM((1, rows), jnp.int32),
            pltpu.VMEM((rows, dpiece), bf16),
            pltpu.VMEM((dpiece, kout), bf16),
            pltpu.VMEM((nten, rows, kpiece), bf16),
            pltpu.VMEM((rows, kout), bf16),
            pltpu.VMEM((dpiece // tile, rows, tile), f32),
            pltpu.VMEM((slots, rank, dpiece), bf16),
            pltpu.VMEM((slots, rank, kpiece), bf16),
            pltpu.VMEM((2, nten, rank, rows), f32),
            pltpu.VMEM((dpiece // tile, rows, tile), bf16),
            pltpu.VMEM((ndp, own, rank, kpiece), bf16),
            pltpu.VMEM((ndp, own, rank, kpiece), bf16),
            dma((7,)),
            dma((nten,)),
            dma((dpiece // tile,)),
            dma((3, slots)),
            dma((slots,)),
            dma((ndp,)),
            dma((ndp,)),
            dma((nten, nblk)),
            dma((nx, nblk)),
            dma((nten, nblk)),
            dma((2, nten)),
            dma((2, nten)),
            dma((ndp,)),
            dma((ndp,)),
        ],
        cost_estimate=pl.CostEstimate(
            flops=2 * rows * dpiece * (kout + 2 * rank),
            bytes_accessed=2 * (2 * rows * dpiece + dpiece * kout + rows * kpiece),
            transcendentals=0,
        ),
        compiler_params=pltpu.CompilerParams(
            collective_id=0, has_side_effects=True, vmem_limit_bytes=64 * 2**20 - 2**18
        ),
    )(
        owner_map, block_adapter, token_adapter.reshape(1, rows), inputs, cotangent, base_weight,
        jnp.swapaxes(down_a, 1, 2), up_b,
    )
    return pl.pallas_call(
        hand_over,
        out_shape=tuple(jax.ShapeDtypeStruct(r.shape, r.dtype) for r in results),
        in_specs=[hbm] * 2,
        out_specs=(hbm, hbm),
        scratch_shapes=[
            pltpu.VMEM((rows, dpiece), bf16),
            pltpu.VMEM((own, rank, kpiece), f32),
            dma((nblk + 1,)),
            dma((nblk + 1,)),
        ],
        cost_estimate=pl.CostEstimate(
            flops=0, bytes_accessed=4 * rows * dpiece, transcendentals=0
        ),
        compiler_params=pltpu.CompilerParams(vmem_limit_bytes=64 * 2**20 - 2**18),
    )(*results)


def solution(mesh):
    in_specs = (
        P("dp", "tensor"),
        P("dp", "tensor"),
        P("tensor", None),
        P("dp", "tensor", None),
        P("dp", None, "tensor"),
        P("dp"),
        P("dp"),
        P(),
    )
    out_specs = (P("dp", "tensor"), P("dp", None, "tensor"))
    return jax.shard_map(
        functools.partial(on_device, mesh.shape["dp"], mesh.shape["tensor"]),
        mesh=mesh, in_specs=in_specs, out_specs=out_specs, check_vma=False,
    )
```

```python
import functools

import jax
import jax.numpy as jnp
from jax import lax
from jax.experimental import pallas as pl
from jax.experimental.pallas import tpu as pltpu
from jax.sharding import PartitionSpec as P

adapter_scale_factor = 2.0
MESH = pl.DeviceIdType.MESH
LAST = (((1,), (1,)), ((), ()))
FIRST = (((0,), (0,)), ((), ()))


def loop(lo, hi, body):
    if hi - lo <= 8:
        for i in range(lo, hi):
            body(i)
    else:
        lax.fori_loop(lo, hi, lambda i, c: (body(i), c)[1], 0)


def kernel(
    ndp, nten, owner_ref, block_ref, tok_ref, x_ref, g_ref, w_ref, a_ref, u_ref,
    out_ref, grad_ref,
    owner, block, tok, xv, wv, gall, gm, acc, aall, uall, part, outv, gsend, grecv,
    local_sem, w_sem, out_sem, a_send, a_recv, u_send, u_recv, g_send, g_fwd, g_recv,
    p_send, p_recv, r_send, r_recv,
):
    nblk = block_ref.shape[0]
    rows, dpiece = x_ref.shape
    kpiece = g_ref.shape[1]
    brows = rows // nblk
    own = a_ref.shape[0]
    inner = 2 if ndp % 2 == 0 else 1
    outer = ndp // inner
    nx = nten // 2
    tiles, _, tile = acc.shape
    me, t = lax.axis_index("dp"), lax.axis_index("tensor")
    z, y = lax.div(me, inner), lax.rem(me, inner)
    xx, c = lax.div(t, 2), lax.rem(t, 2)

    def ten_of(rel):
        core = c if rel % 2 == 0 else 1 - c
        return 2 * lax.rem(xx + rel // 2, nx) + core

    def place_there(rel):
        return 2 * ((nx - rel // 2) % nx) + rel % 2

    barrier = pltpu.get_barrier_semaphore()

    def greet_dp(j):
        pl.semaphore_signal(
            barrier, inc=1, device_id=(lax.rem(me + j, ndp), t), device_id_type=MESH
        )

    def greet_ten(j):
        pl.semaphore_signal(
            barrier, inc=1, device_id=(me, lax.rem(t + j, nten)), device_id_type=MESH
        )

    loop(1, ndp, greet_dp)
    loop(1, nten, greet_ten)

    mine = pl.ds(me * own, own)
    local = [
        pltpu.make_async_copy(src, dst, local_sem.at[i])
        for i, (src, dst) in enumerate((
            (tok_ref, tok), (g_ref, gall.at[0]), (owner_ref, owner), (block_ref, block),
            (u_ref, uall.at[mine]), (a_ref, aall.at[mine]), (x_ref, xv),
        ))
    ]
    weights = [
        pltpu.make_async_copy(
            w_ref.at[:, pl.ds(pl.multiple_of(ten_of(rel) * kpiece, kpiece), kpiece)],
            wv.at[:, pl.ds(rel * kpiece, kpiece)], w_sem.at[rel],
        )
        for rel in range(nten)
    ]
    for cp in local[:2] + weights[:1] + local[2:] + weights[1:]:
        cp.start()
    pl.semaphore_wait(barrier, ndp + nten - 2)

    def hop(src, k, way, first):
        slot = src * own + k
        if way == 2:
            to = inner * z + 1 - y
        else:
            to = inner * (z + 1 - 2 * way) + y
        return pltpu.make_async_remote_copy(
            src_ref=(a_ref.at[k] if first else aall.at[slot]),
            dst_ref=aall.at[slot],
            send_sem=a_send.at[way, slot],
            recv_sem=a_recv.at[slot],
            device_id=(to, t),
            device_id_type=MESH,
        )

    def to_peer(j):
        return pltpu.make_async_remote_copy(
            src_ref=u_ref,
            dst_ref=uall.at[mine],
            send_sem=u_send.at[j],
            recv_sem=u_recv.at[j],
            device_id=(lax.rem(me + j, ndp), t),
            device_id_type=MESH,
        )

    def from_peer(j):
        at = pl.ds(lax.rem(me + ndp - j, ndp) * own, own)
        pltpu.make_async_remote_copy(
            src_ref=u_ref,
            dst_ref=uall.at[at],
            send_sem=u_send.at[j],
            recv_sem=u_recv.at[j],
            device_id=(lax.rem(me + j, ndp), t),
            device_id_type=MESH,
        ).wait_recv()

    def for_ways(fn, ways):
        for way in ways:
            if way == 2:
                if inner == 2:
                    fn(2)
            else:
                ok = z + 1 < outer if way == 0 else z > 0
                pl.when(ok)(functools.partial(fn, way))

    def start_hops(src, k, ways, first=False):
        for_ways(lambda way: hop(src, k, way, first).start(), ways)

    def wait_hops(src, k, ways, first=False):
        for_ways(lambda way: hop(src, k, way, first).wait_send(), ways)

    def got_hop(src, k):
        hop(src, k, 0, False).wait_recv()

    def line(d, k, fn):
        pl.when(z - d >= 0)(lambda: fn(inner * (z - d) + y, k, (0, 2)))
        pl.when(z + d < outer)(lambda: fn(inner * (z + d) + y, k, (1, 2)))

    def lines(d, fn):
        for k in range(own):
            line(d, k, fn)

    def span_of(i):
        return pl.ds(i * brows, brows)

    def g_own(rel, i):
        there = place_there(rel)
        return pltpu.make_async_remote_copy(
            src_ref=g_ref.at[span_of(i)],
            dst_ref=gall.at[there, span_of(i)],
            send_sem=g_send.at[rel, i],
            recv_sem=g_recv.at[there, i],
            device_id=(me, ten_of(rel)),
            device_id_type=MESH,
        )

    def g_pass(j, i):
        return pltpu.make_async_remote_copy(
            src_ref=gall.at[2 * j, span_of(i)],
            dst_ref=gall.at[2 * j + 1, span_of(i)],
            send_sem=g_fwd.at[j, i],
            recv_sem=g_recv.at[2 * j + 1, i],
            device_id=(me, ten_of(1)),
            device_id_type=MESH,
        )

    def g_wait(place, i):
        pltpu.make_async_remote_copy(
            src_ref=gall.at[place, span_of(i)],
            dst_ref=gall.at[place, span_of(i)],
            send_sem=g_send.at[0, i],
            recv_sem=g_recv.at[place, i],
            device_id=(me, ten_of(1)),
            device_id_type=MESH,
        ).wait_recv()

    for k in range(own):
        start_hops(me, k, (0, 1, 2), True)
    for i in range(nblk):
        g_own(1, i).start()

    def send_across(i):
        for j in range(1, nx):
            g_own(2 * j, i).start()

    send_across(0)

    local[0].wait()
    live = (tok[...] >= 0).astype(jnp.float32)
    tall = []
    for b in range(nblk):
        lane = live[:, b * brows:(b + 1) * brows]
        col = jnp.broadcast_to(lane, (brows, brows)).T.astype(jnp.bfloat16)
        reps = -(-kpiece // brows)
        tall.append(jnp.concatenate([col] * reps, axis=1)[:, :kpiece])

    def mask_piece(rel):
        for b in range(nblk):
            gm[span_of(b), rel * kpiece:(rel + 1) * kpiece] = gall[rel, span_of(b), :] * tall[b]

    near = 2 * kpiece

    def product(cols, lo, hi):
        return lax.dot_general(
            gm[:, lo:hi], wv[cols, lo:hi], LAST, preferred_element_type=jnp.float32
        )

    def near_product():
        for i in range(nblk):
            g_wait(1, i)
        mask_piece(1)
        for cp in weights[:2]:
            cp.wait()

        def one(n, carry):
            cols = pl.ds(pl.multiple_of(n * tile, tile), tile)
            acc[n] = product(cols, 0, near)
            return carry

        lax.fori_loop(0, tiles, one, 0)

    local[1].wait()
    mask_piece(0)

    def pass_on(src, k, ways):
        got_hop(src, k)
        start_hops(src, k, ways)

    def pass_g(i):
        for j in range(1, nx):
            g_wait(2 * j, i)
            g_pass(j, i).start()

    if outer <= nblk:
        for d in range(1, outer):
            lines(d, pass_on)
            send_across(d)
        for i in range(outer, nblk):
            send_across(i)
    else:
        for i in range(1, nblk):
            send_across(i)
        loop(1, outer, lambda d: lines(d, pass_on))
    loop(1, ndp, lambda j: to_peer(j).start())
    near_product()

    for cp in local[2:]:
        cp.wait()
    slots = [owner[block[b]] for b in range(nblk)]
    if inner == 2:
        for k in range(own):
            loop(0, outer, lambda d: got_hop(inner * d + 1 - y, k))

    def to_ten(which, rel):
        return pltpu.make_async_remote_copy(
            src_ref=part.at[which, 0], dst_ref=part.at[which, place_there(rel)],
            send_sem=p_send.at[which, rel], recv_sem=p_recv.at[which, place_there(rel)],
            device_id=(me, ten_of(rel)), device_id_type=MESH,
        )

    def from_ten(which, rel):
        pltpu.make_async_remote_copy(
            src_ref=part.at[which, 0], dst_ref=part.at[which, rel],
            send_sem=p_send.at[which, rel], recv_sem=p_recv.at[which, rel],
            device_id=(me, ten_of(rel)), device_id_type=MESH,
        ).wait_recv()

    for which, (pieces, act) in enumerate(((aall, xv), (uall, gall.at[0]))):
        if which == 1:
            loop(1, ndp, from_peer)
        for b in range(nblk):
            span = slice(b * brows, (b + 1) * brows)
            part[which, 0, :, span] = lax.dot_general(
                pieces[slots[b]], act[span, :], LAST, preferred_element_type=jnp.float32
            )
        for rel in range(nten - 1, 0, -1):
            to_ten(which, rel).start()

    for i in range(nblk):
        pass_g(i)
    for j in range(1, nx):
        mask_piece(2 * j)

    def summed(which):
        total = part[which, 0]
        for rel in range(1, nten):
            from_ten(which, rel)
            total = total + part[which, rel]
        return total * live

    lowrank = summed(0).astype(jnp.bfloat16)

    terms = []
    for b in range(nblk):
        span = slice(b * brows, (b + 1) * brows)
        terms.append(
            adapter_scale_factor
            * jnp.dot(lowrank[:, span], gm[span, :kpiece], preferred_element_type=jnp.float32)
        )

    def share(dev, s):
        got = jnp.zeros_like(terms[0])
        for b in range(nblk):
            got = got + jnp.where(slots[b] == dev * own + s, terms[b], 0.0)
        return got

    def to_owner(j):
        return pltpu.make_async_remote_copy(
            src_ref=gsend.at[j], dst_ref=grecv.at[j],
            send_sem=r_send.at[j], recv_sem=r_recv.at[j],
            device_id=(lax.rem(me + j, ndp), t), device_id_type=MESH,
        )

    def scatter(j):
        for s in range(own):
            gsend[j, s] = share(lax.rem(me + j, ndp), s).astype(jnp.bfloat16)
        to_owner(j).start()

    loop(1, ndp, scatter)
    for s in range(own):
        grad_ref[s] = share(me, s)

    for j in range(1, nx):
        for i in range(nblk):
            g_wait(2 * j + 1, i)
        mask_piece(2 * j + 1)
    for cp in weights[2:]:
        cp.wait()
    hidden = summed(1)
    scaled = [
        hidden[:, b * brows:(b + 1) * brows].T.astype(jnp.bfloat16)
        * jnp.bfloat16(adapter_scale_factor)
        for b in range(nblk)
    ]
    kout = wv.shape[1]

    def to_out(n):
        cols = pl.ds(pl.multiple_of(n * tile, tile), tile)
        return pltpu.make_async_copy(outv.at[n], out_ref.at[:, cols], out_sem.at[n])

    def last(n, carry):
        cols = pl.ds(pl.multiple_of(n * tile, tile), tile)
        base = acc[n] + product(cols, near, kout) if nx > 1 else acc[n]
        for b in range(nblk):
            span = slice(b * brows, (b + 1) * brows)
            low = jnp.dot(scaled[b], aall[slots[b], :, cols], preferred_element_type=jnp.float32)
            outv[n, span, :] = (base[span] + low).astype(jnp.bfloat16)
        to_out(n).start()
        return carry

    lax.fori_loop(0, tiles, last, 0)

    for k in range(own):
        wait_hops(me, k, (0, 1, 2), True)
    loop(1, outer, lambda d: lines(d, wait_hops))
    loop(1, ndp, lambda j: to_peer(j).wait_send())
    for i in range(nblk):
        for j in range(1, nx):
            g_own(2 * j, i).wait_send()
            g_pass(j, i).wait_send()
        g_own(1, i).wait_send()
    for which in range(2):
        for rel in range(1, nten):
            to_ten(which, rel).wait_send()

    def gather_grad(j):
        to_owner(j).wait_recv()
        grad_ref[...] += grecv[j].astype(jnp.float32)

    loop(1, ndp, gather_grad)
    loop(1, ndp, lambda j: to_owner(j).wait_send())
    for n in range(tiles):
        to_out(n).wait()


def hand_over(out_ref, grad_ref, out_to, grad_to, out_held, grad_held, sem_in, sem_out):
    parts = sem_in.shape[0] - 1
    rows = out_ref.shape[0] // parts
    ways = [(grad_ref, grad_held, grad_to)]
    for i in range(parts):
        at = pl.ds(i * rows, rows)
        ways.append((out_ref.at[at], out_held.at[at], out_to.at[at]))
    ins = [pltpu.make_async_copy(a, b, sem_in.at[i]) for i, (a, b, _) in enumerate(ways)]
    outs = [pltpu.make_async_copy(b, c, sem_out.at[i]) for i, (_, b, c) in enumerate(ways)]
    for cp in ins:
        cp.start()
    for cp, then in zip(ins, outs):
        cp.wait()
        then.start()
    for cp in outs:
        cp.wait()


def on_device(
    ndp, nten, inputs, cotangent, base_weight, down_a, up_b, block_adapter, token_adapter, owner_map
):
    rows, dpiece = inputs.shape
    kpiece = cotangent.shape[1]
    nblk = block_adapter.shape[0]
    own, rank = up_b.shape[:2]
    slots = own * ndp
    kout = base_weight.shape[1]
    nx = nten // 2
    tile = 256 if dpiece % 256 == 0 else 128
    bf16, f32 = jnp.bfloat16, jnp.float32
    hbm = pl.BlockSpec(memory_space=pltpu.HBM)
    dma = pltpu.SemaphoreType.DMA
    results = pl.pallas_call(
        functools.partial(kernel, ndp, nten),
        out_shape=(
            jax.ShapeDtypeStruct((rows, dpiece), bf16),
            jax.ShapeDtypeStruct((own, rank, kpiece), f32),
        ),
        in_specs=[hbm] * 8,
        out_specs=(pl.BlockSpec(memory_space=pl.ANY), pl.BlockSpec(memory_space=pltpu.VMEM)),
        scratch_shapes=[
            pltpu.SMEM(owner_map.shape, jnp.int32),
            pltpu.SMEM((nblk,), jnp.int32),
            pltpu.VMEM((1, rows), jnp.int32),
            pltpu.VMEM((rows, dpiece), bf16),
            pltpu.VMEM((dpiece, kout), bf16),
            pltpu.VMEM((nten, rows, kpiece), bf16),
            pltpu.VMEM((rows, kout), bf16),
            pltpu.VMEM((dpiece // tile, rows, tile), f32),
            pltpu.VMEM((slots, rank, dpiece), bf16),
            pltpu.VMEM((slots, rank, kpiece), bf16),
            pltpu.VMEM((2, nten, rank, rows), f32),
            pltpu.VMEM((dpiece // tile, rows, tile), bf16),
            pltpu.VMEM((ndp, own, rank, kpiece), bf16),
            pltpu.VMEM((ndp, own, rank, kpiece), bf16),
            dma((7,)),
            dma((nten,)),
            dma((dpiece // tile,)),
            dma((3, slots)),
            dma((slots,)),
            dma((ndp,)),
            dma((ndp,)),
            dma((nten, nblk)),
            dma((nx, nblk)),
            dma((nten, nblk)),
            dma((2, nten)),
            dma((2, nten)),
            dma((ndp,)),
            dma((ndp,)),
        ],
        cost_estimate=pl.CostEstimate(
            flops=2 * rows * dpiece * (kout + 2 * rank),
            bytes_accessed=2 * (2 * rows * dpiece + dpiece * kout + rows * kpiece),
            transcendentals=0,
        ),
        compiler_params=pltpu.CompilerParams(
            collective_id=0, has_side_effects=True, vmem_limit_bytes=64 * 2**20 - 2**18
        ),
    )(
        owner_map, block_adapter, token_adapter.reshape(1, rows), inputs, cotangent, base_weight,
        jnp.swapaxes(down_a, 1, 2), up_b,
    )
    return pl.pallas_call(
        hand_over,
        out_shape=tuple(jax.ShapeDtypeStruct(r.shape, r.dtype) for r in results),
        in_specs=[hbm] * 2,
        out_specs=(hbm, hbm),
        scratch_shapes=[
            pltpu.VMEM((rows, dpiece), bf16),
            pltpu.VMEM((own, rank, kpiece), f32),
            dma((nblk + 1,)),
            dma((nblk + 1,)),
        ],
        cost_estimate=pl.CostEstimate(
            flops=0, bytes_accessed=4 * rows * dpiece, transcendentals=0
        ),
        compiler_params=pltpu.CompilerParams(vmem_limit_bytes=64 * 2**20 - 2**18),
    )(*results)


def solution(mesh):
    in_specs = (
        P("dp", "tensor"),
        P("dp", "tensor"),
        P("tensor", None),
        P("dp", "tensor", None),
        P("dp", None, "tensor"),
        P("dp"),
        P("dp"),
        P(),
    )
    out_specs = (P("dp", "tensor"), P("dp", None, "tensor"))
    return jax.shard_map(
        functools.partial(on_device, mesh.shape["dp"], mesh.shape["tensor"]),
        mesh=mesh, in_specs=in_specs, out_specs=out_specs, check_vma=False,
    )
```

```python
import functools

import jax
import jax.numpy as jnp
from jax import lax
from jax.experimental import pallas as pl
from jax.experimental.pallas import tpu as pltpu
from jax.sharding import PartitionSpec as P

adapter_scale_factor = 2.0
MESH = pl.DeviceIdType.MESH
LAST = (((1,), (1,)), ((), ()))
FIRST = (((0,), (0,)), ((), ()))


def loop(lo, hi, body):
    if hi - lo <= 8:
        for i in range(lo, hi):
            body(i)
    else:
        lax.fori_loop(lo, hi, lambda i, c: (body(i), c)[1], 0)


def kernel(
    ndp, nten, owner_ref, block_ref, tok_ref, x_ref, g_ref, w_ref, a_ref, u_ref,
    out_ref, grad_ref,
    owner, block, tok, xv, wv, gall, gm, acc, aall, uall, part, outv, gsend, grecv,
    local_sem, w_sem, out_sem, a_send, a_recv, u_send, u_recv, g_send, g_fwd, g_recv,
    p_send, p_recv, r_send, r_recv,
):
    nblk = block_ref.shape[0]
    rows, dpiece = x_ref.shape
    kpiece = g_ref.shape[1]
    brows = rows // nblk
    own = a_ref.shape[0]
    inner = 2 if ndp % 2 == 0 else 1
    outer = ndp // inner
    nx = nten // 2
    tiles, _, tile = acc.shape
    me, t = lax.axis_index("dp"), lax.axis_index("tensor")
    z, y = lax.div(me, inner), lax.rem(me, inner)
    xx, c = lax.div(t, 2), lax.rem(t, 2)

    def ten_of(rel):
        core = c if rel % 2 == 0 else 1 - c
        return 2 * lax.rem(xx + rel // 2, nx) + core

    def place_there(rel):
        return 2 * ((nx - rel // 2) % nx) + rel % 2

    barrier = pltpu.get_barrier_semaphore()

    def greet_dp(j):
        pl.semaphore_signal(
            barrier, inc=1, device_id=(lax.rem(me + j, ndp), t), device_id_type=MESH
        )

    def greet_ten(j):
        pl.semaphore_signal(
            barrier, inc=1, device_id=(me, lax.rem(t + j, nten)), device_id_type=MESH
        )

    loop(1, ndp, greet_dp)
    loop(1, nten, greet_ten)

    mine = pl.ds(me * own, own)
    local = [
        pltpu.make_async_copy(src, dst, local_sem.at[i])
        for i, (src, dst) in enumerate((
            (tok_ref, tok), (g_ref, gall.at[0]), (owner_ref, owner), (block_ref, block),
            (u_ref, uall.at[mine]), (a_ref, aall.at[mine]), (x_ref, xv),
        ))
    ]
    weights = [
        pltpu.make_async_copy(
            w_ref.at[:, pl.ds(pl.multiple_of(ten_of(rel) * kpiece, kpiece), kpiece)],
            wv.at[:, pl.ds(rel * kpiece, kpiece)], w_sem.at[rel],
        )
        for rel in range(nten)
    ]
    for cp in local[:2] + weights[:1] + local[2:] + weights[1:]:
        cp.start()
    pl.semaphore_wait(barrier, ndp + nten - 2)

    def hop(src, k, way, first):
        slot = src * own + k
        if way == 2:
            to = inner * z + 1 - y
        else:
            to = inner * (z + 1 - 2 * way) + y
        return pltpu.make_async_remote_copy(
            src_ref=(a_ref.at[k] if first else aall.at[slot]),
            dst_ref=aall.at[slot],
            send_sem=a_send.at[way, slot],
            recv_sem=a_recv.at[slot],
            device_id=(to, t),
            device_id_type=MESH,
        )

    def u_copy(which, j, src, dev, owner):
        return pltpu.make_async_remote_copy(
            src_ref=src,
            dst_ref=uall.at[pl.ds(owner * own, own)],
            send_sem=u_send.at[which * outer + j],
            recv_sem=u_recv.at[which * outer + j],
            device_id=(dev, t),
            device_id_type=MESH,
        )

    pair = inner * z + inner - 1 - y

    def u_hop(which, j):
        if which == 0:
            src, owner = u_ref, me
        else:
            src, owner = uall.at[pl.ds(pair * own, own)], pair
        dev = inner * lax.rem(z + j, outer) + y
        return u_copy(which, j, src, dev, owner)

    def u_pair():
        return u_copy(0, 0, u_ref, pair, me)

    def u_wait(which, j):
        row = y if which == 0 else inner - 1 - y
        owner = inner * lax.rem(z + outer - j, outer) + row
        u_copy(which, j, u_ref, pair, owner).wait_recv()

    def u_all(which, fn):
        loop(1, outer, lambda j: fn(which, j))

    def u_start(which, j):
        u_hop(which, j).start()

    def u_left(which, j):
        u_hop(which, j).wait_send()

    def for_ways(fn, ways):
        for way in ways:
            if way == 2:
                if inner == 2:
                    fn(2)
            else:
                ok = z + 1 < outer if way == 0 else z > 0
                pl.when(ok)(functools.partial(fn, way))

    def start_hops(src, k, ways, first=False):
        for_ways(lambda way: hop(src, k, way, first).start(), ways)

    def wait_hops(src, k, ways, first=False):
        for_ways(lambda way: hop(src, k, way, first).wait_send(), ways)

    def got_hop(src, k):
        hop(src, k, 0, False).wait_recv()

    def line(d, k, fn):
        pl.when(z - d >= 0)(lambda: fn(inner * (z - d) + y, k, (0, 2)))
        pl.when(z + d < outer)(lambda: fn(inner * (z + d) + y, k, (1, 2)))

    def lines(d, fn):
        for k in range(own):
            line(d, k, fn)

    def span_of(i):
        return pl.ds(i * brows, brows)

    def g_own(rel, i):
        there = place_there(rel)
        return pltpu.make_async_remote_copy(
            src_ref=g_ref.at[span_of(i)],
            dst_ref=gall.at[there, span_of(i)],
            send_sem=g_send.at[rel, i],
            recv_sem=g_recv.at[there, i],
            device_id=(me, ten_of(rel)),
            device_id_type=MESH,
        )

    def g_pass(j, i):
        return pltpu.make_async_remote_copy(
            src_ref=gall.at[2 * j, span_of(i)],
            dst_ref=gall.at[2 * j + 1, span_of(i)],
            send_sem=g_fwd.at[j, i],
            recv_sem=g_recv.at[2 * j + 1, i],
            device_id=(me, ten_of(1)),
            device_id_type=MESH,
        )

    def g_wait(place, i):
        pltpu.make_async_remote_copy(
            src_ref=gall.at[place, span_of(i)],
            dst_ref=gall.at[place, span_of(i)],
            send_sem=g_send.at[0, i],
            recv_sem=g_recv.at[place, i],
            device_id=(me, ten_of(1)),
            device_id_type=MESH,
        ).wait_recv()

    for k in range(own):
        start_hops(me, k, (0, 1), True)
        if k == 0:
            if inner == 2:
                u_pair().start()
            u_all(0, u_start)
        start_hops(me, k, (2,), True)
    for i in range(nblk):
        g_own(1, i).start()

    def send_across(i):
        for j in range(1, nx):
            g_own(2 * j, i).start()

    send_across(0)

    local[0].wait()
    live = (tok[...] >= 0).astype(jnp.float32)
    tall = []
    for b in range(nblk):
        lane = live[:, b * brows:(b + 1) * brows]
        col = jnp.broadcast_to(lane, (brows, brows)).T.astype(jnp.bfloat16)
        reps = -(-kpiece // brows)
        tall.append(jnp.concatenate([col] * reps, axis=1)[:, :kpiece])

    def mask_piece(rel):
        for b in range(nblk):
            gm[span_of(b), rel * kpiece:(rel + 1) * kpiece] = gall[rel, span_of(b), :] * tall[b]

    near = 2 * kpiece

    def product(cols, lo, hi):
        return lax.dot_general(
            gm[:, lo:hi], wv[cols, lo:hi], LAST, preferred_element_type=jnp.float32
        )

    def near_product():
        for i in range(nblk):
            g_wait(1, i)
        mask_piece(1)
        for cp in weights[:2]:
            cp.wait()

        def one(n, carry):
            cols = pl.ds(pl.multiple_of(n * tile, tile), tile)
            acc[n] = product(cols, 0, near)
            return carry

        lax.fori_loop(0, tiles, one, 0)

    local[1].wait()
    mask_piece(0)

    def pass_on(src, k, ways):
        got_hop(src, k)
        start_hops(src, k, ways)

    def pass_g(i):
        for j in range(1, nx):
            g_wait(2 * j, i)
            g_pass(j, i).start()

    def u_relay():
        if inner == 2:
            u_copy(0, 0, u_ref, pair, pair).wait_recv()
            u_all(1, u_start)

    if outer <= nblk:
        if outer == 1:
            u_relay()
        for d in range(1, outer):
            lines(d, pass_on)
            send_across(d)
            if d == 1:
                u_relay()
        for i in range(outer, nblk):
            send_across(i)
    else:
        for i in range(1, nblk):
            send_across(i)
        u_relay()
        loop(1, outer, lambda d: lines(d, pass_on))
    near_product()

    for cp in local[2:]:
        cp.wait()
    slots = [owner[block[b]] for b in range(nblk)]
    def to_ten(which, rel):
        return pltpu.make_async_remote_copy(
            src_ref=part.at[which, 0], dst_ref=part.at[which, place_there(rel)],
            send_sem=p_send.at[which, rel], recv_sem=p_recv.at[which, place_there(rel)],
            device_id=(me, ten_of(rel)), device_id_type=MESH,
        )

    def from_ten(which, rel):
        pltpu.make_async_remote_copy(
            src_ref=part.at[which, 0], dst_ref=part.at[which, rel],
            send_sem=p_send.at[which, rel], recv_sem=p_recv.at[which, rel],
            device_id=(me, ten_of(rel)), device_id_type=MESH,
        ).wait_recv()

    def send_partial(which, pieces, act):
        for b in range(nblk):
            span = slice(b * brows, (b + 1) * brows)
            part[which, 0, :, span] = lax.dot_general(
                pieces[slots[b]], act[span, :], LAST, preferred_element_type=jnp.float32
            )
        for rel in range(nten - 1, 0, -1):
            to_ten(which, rel).start()

    u_all(0, u_wait)
    if inner == 2:
        u_all(1, u_wait)
    send_partial(1, uall, gall.at[0])
    if inner == 2:
        for k in range(own):
            loop(0, outer, lambda d: got_hop(inner * d + 1 - y, k))

    send_partial(0, aall, xv)

    for i in range(nblk):
        pass_g(i)
    for j in range(1, nx):
        mask_piece(2 * j)

    def summed(which):
        total = part[which, 0]
        for rel in range(1, nten):
            from_ten(which, rel)
            total = total + part[which, rel]
        return total * live

    lowrank = summed(0).astype(jnp.bfloat16)

    terms = []
    for b in range(nblk):
        span = slice(b * brows, (b + 1) * brows)
        terms.append(
            adapter_scale_factor
            * jnp.dot(lowrank[:, span], gm[span, :kpiece], preferred_element_type=jnp.float32)
        )

    def share(dev, s):
        got = jnp.zeros_like(terms[0])
        for b in range(nblk):
            got = got + jnp.where(slots[b] == dev * own + s, terms[b], 0.0)
        return got

    def to_owner(j):
        return pltpu.make_async_remote_copy(
            src_ref=gsend.at[j], dst_ref=grecv.at[j],
            send_sem=r_send.at[j], recv_sem=r_recv.at[j],
            device_id=(lax.rem(me + j, ndp), t), device_id_type=MESH,
        )

    def scatter(j):
        for s in range(own):
            gsend[j, s] = share(lax.rem(me + j, ndp), s).astype(jnp.bfloat16)
        to_owner(j).start()

    loop(1, ndp, scatter)
    for s in range(own):
        grad_ref[s] = share(me, s)

    for j in range(1, nx):
        for i in range(nblk):
            g_wait(2 * j + 1, i)
        mask_piece(2 * j + 1)
    for cp in weights[2:]:
        cp.wait()
    hidden = summed(1)
    scaled = [
        hidden[:, b * brows:(b + 1) * brows].T.astype(jnp.bfloat16)
        * jnp.bfloat16(adapter_scale_factor)
        for b in range(nblk)
    ]
    kout = wv.shape[1]

    def to_out(n):
        cols = pl.ds(pl.multiple_of(n * tile, tile), tile)
        return pltpu.make_async_copy(outv.at[n], out_ref.at[:, cols], out_sem.at[n])

    def last(n, carry):
        cols = pl.ds(pl.multiple_of(n * tile, tile), tile)
        base = acc[n] + product(cols, near, kout) if nx > 1 else acc[n]
        for b in range(nblk):
            span = slice(b * brows, (b + 1) * brows)
            low = jnp.dot(scaled[b], aall[slots[b], :, cols], preferred_element_type=jnp.float32)
            outv[n, span, :] = (base[span] + low).astype(jnp.bfloat16)
        to_out(n).start()
        return carry

    lax.fori_loop(0, tiles, last, 0)

    for k in range(own):
        wait_hops(me, k, (0, 1, 2), True)
    loop(1, outer, lambda d: lines(d, wait_hops))
    u_all(0, u_left)
    if inner == 2:
        u_pair().wait_send()
        u_all(1, u_left)
    for i in range(nblk):
        for j in range(1, nx):
            g_own(2 * j, i).wait_send()
            g_pass(j, i).wait_send()
        g_own(1, i).wait_send()
    for which in range(2):
        for rel in range(1, nten):
            to_ten(which, rel).wait_send()

    def gather_grad(j):
        to_owner(j).wait_recv()
        grad_ref[...] += grecv[j].astype(jnp.float32)

    loop(1, ndp, gather_grad)
    loop(1, ndp, lambda j: to_owner(j).wait_send())
    for n in range(tiles):
        to_out(n).wait()


def hand_over(out_ref, grad_ref, out_to, grad_to, out_held, grad_held, sem_in, sem_out):
    parts = sem_in.shape[0] - 1
    rows = out_ref.shape[0] // parts
    ways = [(grad_ref, grad_held, grad_to)]
    for i in range(parts):
        at = pl.ds(i * rows, rows)
        ways.append((out_ref.at[at], out_held.at[at], out_to.at[at]))
    ins = [pltpu.make_async_copy(a, b, sem_in.at[i]) for i, (a, b, _) in enumerate(ways)]
    outs = [pltpu.make_async_copy(b, c, sem_out.at[i]) for i, (_, b, c) in enumerate(ways)]
    for cp in ins:
        cp.start()
    for cp, then in zip(ins, outs):
        cp.wait()
        then.start()
    for cp in outs:
        cp.wait()


def on_device(
    ndp, nten, inputs, cotangent, base_weight, down_a, up_b, block_adapter, token_adapter, owner_map
):
    rows, dpiece = inputs.shape
    kpiece = cotangent.shape[1]
    nblk = block_adapter.shape[0]
    own, rank = up_b.shape[:2]
    slots = own * ndp
    kout = base_weight.shape[1]
    nx = nten // 2
    tile = 256 if dpiece % 256 == 0 else 128
    bf16, f32 = jnp.bfloat16, jnp.float32
    hbm = pl.BlockSpec(memory_space=pltpu.HBM)
    dma = pltpu.SemaphoreType.DMA
    results = pl.pallas_call(
        functools.partial(kernel, ndp, nten),
        out_shape=(
            jax.ShapeDtypeStruct((rows, dpiece), bf16),
            jax.ShapeDtypeStruct((own, rank, kpiece), f32),
        ),
        in_specs=[hbm] * 8,
        out_specs=(pl.BlockSpec(memory_space=pl.ANY), pl.BlockSpec(memory_space=pltpu.VMEM)),
        scratch_shapes=[
            pltpu.SMEM(owner_map.shape, jnp.int32),
            pltpu.SMEM((nblk,), jnp.int32),
            pltpu.VMEM((1, rows), jnp.int32),
            pltpu.VMEM((rows, dpiece), bf16),
            pltpu.VMEM((dpiece, kout), bf16),
            pltpu.VMEM((nten, rows, kpiece), bf16),
            pltpu.VMEM((rows, kout), bf16),
            pltpu.VMEM((dpiece // tile, rows, tile), f32),
            pltpu.VMEM((slots, rank, dpiece), bf16),
            pltpu.VMEM((slots, rank, kpiece), bf16),
            pltpu.VMEM((2, nten, rank, rows), f32),
            pltpu.VMEM((dpiece // tile, rows, tile), bf16),
            pltpu.VMEM((ndp, own, rank, kpiece), bf16),
            pltpu.VMEM((ndp, own, rank, kpiece), bf16),
            dma((7,)),
            dma((nten,)),
            dma((dpiece // tile,)),
            dma((3, slots)),
            dma((slots,)),
            dma((ndp,)),
            dma((ndp,)),
            dma((nten, nblk)),
            dma((nx, nblk)),
            dma((nten, nblk)),
            dma((2, nten)),
            dma((2, nten)),
            dma((ndp,)),
            dma((ndp,)),
        ],
        cost_estimate=pl.CostEstimate(
            flops=2 * rows * dpiece * (kout + 2 * rank),
            bytes_accessed=2 * (2 * rows * dpiece + dpiece * kout + rows * kpiece),
            transcendentals=0,
        ),
        compiler_params=pltpu.CompilerParams(
            collective_id=0, has_side_effects=True, vmem_limit_bytes=64 * 2**20 - 2**18
        ),
    )(
        owner_map, block_adapter, token_adapter.reshape(1, rows), inputs, cotangent, base_weight,
        jnp.swapaxes(down_a, 1, 2), up_b,
    )
    return pl.pallas_call(
        hand_over,
        out_shape=tuple(jax.ShapeDtypeStruct(r.shape, r.dtype) for r in results),
        in_specs=[hbm] * 2,
        out_specs=(hbm, hbm),
        scratch_shapes=[
            pltpu.VMEM((rows, dpiece), bf16),
            pltpu.VMEM((own, rank, kpiece), f32),
            dma((nblk + 1,)),
            dma((nblk + 1,)),
        ],
        cost_estimate=pl.CostEstimate(
            flops=0, bytes_accessed=4 * rows * dpiece, transcendentals=0
        ),
        compiler_params=pltpu.CompilerParams(vmem_limit_bytes=64 * 2**20 - 2**18),
    )(*results)


def solution(mesh):
    in_specs = (
        P("dp", "tensor"),
        P("dp", "tensor"),
        P("tensor", None),
        P("dp", "tensor", None),
        P("dp", None, "tensor"),
        P("dp"),
        P("dp"),
        P(),
    )
    out_specs = (P("dp", "tensor"), P("dp", None, "tensor"))
    return jax.shard_map(
        functools.partial(on_device, mesh.shape["dp"], mesh.shape["tensor"]),
        mesh=mesh, in_specs=in_specs, out_specs=out_specs, check_vma=False,
    )
```
